128 devices in a mesh: group: 8 (over z, core), block: 16 (over y, x).
Axes of the slice: x: 4, y: 4, z: 4, core: 2. Of those that a mesh axis runs over, the one named last changes fastest.
Arguments:
- embeddings: float32 [65536, 1024], P(('group', 'block')), may hold values from -6 to 6
- labels: int32 [65536, 1], P(('group', 'block')), may hold values from 0 to 7; in each aligned block of 512 rows (0 to 511, 512 to 1023, ...) at most 96 rows name the same one
- row_ids: int32 [65536], P(('group', 'block')), may hold values from 0 to 65535, each once
Outputs:
- dup_score: float32 [65536], P(('group', 'block'))
The draws below stay inside these ranges and needn't reach their ends.
Inputs may be any that keep to these rules, and one draw needn't show every extreme that they name: `labels`: among the rows of one device (aligned blocks of 512 rows) no cluster appears more than 96 times; some cluster appears exactly 96 times. `row_ids`: every value appears exactly once.
All inputs are finite; a program needn't handle non-finite values.
Results may differ from the reference program's by a relative error of at most 0.0012.
Values may be sent and summed in bfloat16 or wider, within the bound.
No kernel may reach another device: no remote copies, remote signals or barrier semaphores. Data moves between devices by JAX's collectives and lax.ppermute only.
A program may use at most 128 MiB of HBM per device.

```python
import math
import jax
import jax.numpy as jnp
import numpy as np
from jax import lax

D = 1024
ROWS_DEV = 512
CAPACITY = 96
CLUSTERS = 8
TOTAL = 65536


def level_of(stream_key, shape, shards, low, largest):
    def one(position, parts):
        steps = jax.random.uniform(jax.random.fold_in(jax.random.fold_in(stream_key, 6), position), (parts,), jnp.float32, low / len(shards), largest / len(shards))
        return jnp.repeat(jnp.exp(steps), shape[position] // parts).reshape((-1,) + (1,) * (len(shape) - position - 1))

    level = one(*shards[0])
    for cut in shards[1:]:
        level = level * one(*cut)
    return level


def assign_block(key, own, number, rows, number_of, top, most, lean):
    order = jax.random.permutation(key, number_of)
    heavy_load, ordinary = portions_of(number_of, rows * top, most, lean, True), portions_of(number_of, rows * top, most, lean, False)
    places = jnp.arange(number_of)

    def named(tallies, turn):
        used = int((tallies > 0).sum())
        fixed = max(1, used // 4)
        shifted = fixed + (places - fixed + turn * (used - fixed)) % max(1, number_of - fixed)
        return jnp.zeros((number_of,), jnp.int32).at[order[jnp.where(places < fixed, places, shifted)]].set(jnp.asarray(tallies, jnp.int32))

    tallies = jnp.where(number % 4 == 0, named(heavy_load, number // 4), named(ordinary, number - number // 4 - 1))
    mixed = jax.random.permutation(jax.random.fold_in(own, 3), number_of)
    source_of, receiver = mixed[0:number_of // 2 * 2:2], mixed[1:number_of // 2 * 2:2]
    slack = jnp.minimum(tallies[source_of] - 1, most - tallies[receiver]) // 2
    slack = jnp.where((source_of == order[0]) | (receiver == order[0]) | (tallies[receiver] == 0), 0, jnp.maximum(slack, 0))
    shifted = jax.random.randint(jax.random.fold_in(own, 4), (number_of // 2,), 0, 1 << 20) % (slack + 1)
    tallies = tallies.at[source_of].add(-shifted).at[receiver].add(shifted)
    members = jnp.searchsorted(jnp.cumsum(tallies), jnp.arange(rows * top), side="right").astype(jnp.int32)
    table = members.reshape(top, rows).T
    table = table[jax.random.permutation(jax.random.fold_in(own, 1), rows)]
    turn = jax.random.randint(jax.random.fold_in(own, 2), (rows, 1), 0, top)
    return jnp.take_along_axis(table, (jnp.arange(top)[None, :] + turn) % top, axis=1)


def portions_of(number_of, total, most, lean, full):
    weights = [(1 << 20) // math.isqrt(standing ** lean) + 1 for standing in range(1, number_of + 1)]
    largest = most if full else min(most, max(-(-total // number_of), total * weights[0] // sum(weights)))
    least = 1 if total - largest >= number_of - 1 else 0
    counts, surplus = [largest] + [least] * (number_of - 1), total - largest - least * (number_of - 1)
    while surplus > 0:
        free = [i for i in range(1, number_of) if counts[i] < largest] or [i for i in range(1, number_of) if counts[i] < most]
        whole, budget = sum([weights[i] for i in free]), surplus
        for i in free:
            addition = min(most - counts[i], max(1, budget * weights[i] // whole), surplus)
            counts[i] = counts[i] + addition
            surplus = surplus - addition
    return np.array(counts)


def bell_draw(key, extent, scale, limit, shards=(), kind=jnp.bfloat16):
    values = jax.random.normal(key, extent, jnp.float32) * scale
    if len(shards) > 0:
        values = level_of(key, extent, shards, -0.22, 0.18) * values
    return jnp.clip(values, min=-limit, max=limit).astype(kind)


def setup_inputs(seed: int = 0) -> dict:
    seeds = jax.random.split(jax.random.key(seed), 4)
    embeddings = bell_draw(seeds[0], (TOTAL, D), 1.0, 6.0, ((0, 128),), jnp.float32)
    labels_keys = jax.random.split(jax.random.fold_in(seeds[1], 1), TOTAL // ROWS_DEV)
    labels_turns = jax.random.permutation(jax.random.fold_in(seeds[1], 3), TOTAL // ROWS_DEV)
    labels = jax.vmap(lambda own, number: assign_block(jax.random.fold_in(seeds[1], 2), own, number, ROWS_DEV, CLUSTERS, 1, CAPACITY, 2))(labels_keys, labels_turns).reshape((TOTAL, 1))
    row_ids = jax.random.permutation(seeds[2], TOTAL).astype(jnp.int32)
    return dict(embeddings=embeddings, labels=labels, row_ids=row_ids)


def unit_rows(embeddings):
    scale = lax.rsqrt(lax.optimization_barrier(jnp.sum(embeddings * embeddings, axis=1, keepdims=True)) + 1e-06)
    return (embeddings * scale).astype(jnp.bfloat16)

def reference(embeddings, labels, row_ids):
    normed = unit_rows(embeddings)
    row_labels = labels[:, 0]
    total_rows = normed.shape[0]
    features = normed.shape[1]
    sort_key = row_labels * total_rows + row_ids
    order = jnp.argsort(sort_key).astype(jnp.int32)
    sorted_rows = normed[order]
    sorted_labels = row_labels[order]
    span = math.gcd(total_rows, 1024)
    count_blocks = total_rows // span
    block_rows = sorted_rows.reshape(count_blocks, span, features)
    block_labels = sorted_labels.reshape(count_blocks, span)
    offsets = jnp.arange(span, dtype=jnp.int32)

    def one_block(index):
        here_rows = block_rows[index]
        here_labels = block_labels[index]
        here_pos = index * span + offsets

        def visit(other, running):

            def compute(current):
                there_rows = block_rows[other]
                there_labels = block_labels[other]
                there_pos = other * span + offsets
                scores = jnp.dot(here_rows, there_rows.T, preferred_element_type=jnp.float32)
                earlier = (here_labels[:, None] == there_labels[None, :]) & (there_pos[None, :] < here_pos[:, None])
                return jnp.maximum(current, lax.optimization_barrier(jnp.max(jnp.where(earlier, scores, -1.0), axis=1)))
            return lax.cond(block_labels[other, span - 1] >= here_labels[0], compute, lambda current: current, running)
        return lax.fori_loop(0, index + 1, visit, jnp.full((span,), -1.0, jnp.float32))
    result = lax.map(one_block, jnp.arange(count_blocks, dtype=jnp.int32))
    return jnp.zeros((total_rows,), jnp.float32).at[order].set(result.reshape(-1))
```

```python
import functools
import jax
import jax.numpy as jnp
from jax import lax
from jax.experimental import pallas as pl
from jax.experimental.pallas import tpu as pltpu
from jax.sharding import PartitionSpec as P

AXES = ("group", "block")
SIDE = 4
ROWS = 512
FEATURES = 1024
EXTRA = 16
MIB = 1 << 20

EDGES = (
    (0, 0, -1), (0, 1, -1), (0, 2, 1),
    (1, 0, -1), (1, 1, 1), (3, 2, 1),
    (3, 0, 1), (5, 1, 1), (5, 2, -1),
    (8, 0, 1), (1, 1, -1), (8, 2, -1),
)
OWN = len(EDGES) + 1
SHARED = (0, 4, 6, 7)
BLOCKS = OWN + len(SHARED)
TABLE = 24
STAGES = (
    (0, (0,)), (13, (0,)), (1, (0, 13)), (2, (0, 1, 13)), (3, (0, 1, 2)), (4, (0, 2, 3, 13)),
    (5, (2, 3, 4, 13)), (6, (0, 1, 2, 4, 5)), (14, (1, 2, 3, 5)), (15, (2, 5, 6)),
    (7, (2, 5, 6, 13, 14, 15)), (8, (1, 3, 6, 7, 13, 14, 15)), (16, (1, 2, 5, 8)),
    (9, (1, 4, 6, 7, 13, 14, 15, 16)), (10, (3, 4, 6, 13, 15, 16)), (11, (6, 7, 13, 14, 15, 16)),
    (12, (6, 7, 14, 15, 16)),
)


def of_core(core, offset):
    return offset if core == 0 else offset[::-1]


def permutation(offset, swap=False):
    pairs = []
    for z in range(SIDE):
        for core in range(2):
            dx, dy, dz = of_core(core, offset)
            for y in range(SIDE):
                for x in range(SIDE):
                    source = (z * 2 + core) * 16 + y * 4 + x
                    to_core = 1 - core if swap else core
                    target = ((z + dz) % SIDE * 2 + to_core) * 16 + (y + dy) % SIDE * 4 + (x + dx) % SIDE
                    pairs.append((source, target))
    return pairs


def step_of(axis, sign):
    return tuple(sign if a == axis else 0 for a in range(3))


def offsets():
    found = [(0, 0, 0)]
    for parent, axis, sign in EDGES:
        found.append(tuple((a + b) % SIDE for a, b in zip(found[parent], step_of(axis, sign))))
    return found


def column_of(row):
    return jnp.transpose(jnp.broadcast_to(row, (128, row.shape[1])))


def prepare_kernel(emb_ref, label_ref, id_ref, out_ref, rank_ref):
    values = emb_ref[...]
    scale = lax.rsqrt(jnp.sum(values * values, axis=1, keepdims=True) + 1e-06)
    normed = (values * scale).astype(jnp.bfloat16)
    labels = label_ref[...]
    ids = id_ref[...]
    order = labels * ROWS + lax.broadcasted_iota(jnp.int32, (1, ROWS), 1)
    order_column = jnp.concatenate([column_of(order)] * (ROWS // 128), axis=1)
    rank = jnp.sum((order_column < order).astype(jnp.int32), axis=0, keepdims=True)
    rank_ref[...] = rank
    place = (lax.broadcasted_iota(jnp.int32, (ROWS, ROWS), 0) == rank).astype(jnp.bfloat16)
    out_ref[0:ROWS, :] = jnp.dot(place, normed, preferred_element_type=jnp.float32).astype(jnp.bfloat16)
    low = ids & 255
    digits = jnp.concatenate(
        [low.astype(jnp.float32), (ids >> 8).astype(jnp.float32), labels.astype(jnp.float32)]
        + [jnp.zeros((5, ROWS), jnp.float32)], axis=0).astype(jnp.bfloat16)
    digits = lax.dot_general(digits, place, (((1,), (1,)), ((), ())), preferred_element_type=jnp.float32)
    zeros = jnp.zeros((EXTRA - 2, 2 * ROWS), jnp.float32)
    extra = jnp.concatenate([
        jnp.concatenate([digits[0:1], digits[1:2]], axis=1),
        jnp.concatenate([digits[2:3], digits[3:4]], axis=1), zeros], axis=0)
    out_ref[ROWS:ROWS + EXTRA, :] = extra.astype(jnp.bfloat16)


def prepare(embeddings, labels, row_ids):
    return pl.pallas_call(
        prepare_kernel,
        out_shape=(
            jax.ShapeDtypeStruct((ROWS + EXTRA, FEATURES), jnp.bfloat16),
            jax.ShapeDtypeStruct((1, ROWS), jnp.int32),
        ),
        in_specs=[pl.BlockSpec(memory_space=pltpu.VMEM)] * 3,
        out_specs=(pl.BlockSpec(memory_space=pltpu.VMEM),) * 2,
        compiler_params=pltpu.CompilerParams(vmem_limit_bytes=32 * MIB),
        name="prepare",
    )(embeddings, labels, row_ids)


def keys_of(extra):
    digits = extra.astype(jnp.float32)
    ids = (digits[0:1, 0:ROWS] + digits[0:1, ROWS:2 * ROWS] * 256.0).astype(jnp.int32)
    labels = digits[1:2, 0:ROWS].astype(jnp.int32) * 65536
    return labels, ids


def stage_kernel(block, partners, *refs):
    count = len(partners)
    own_pair = partners == (block,)
    copies = 1 if own_pair else count + 1
    sources = refs[:copies]
    where_ref, table_in, table_ref, held, sems = refs[copies:]
    for k in range(copies):
        pltpu.make_async_copy(sources[k], held.at[k], sems.at[k]).start()
    table_ref[...] = table_in[...]
    pltpu.make_async_copy(sources[0], held.at[0], sems.at[0]).wait()
    labels, ids = keys_of(held[0, ROWS:ROWS + EXTRA, :])
    keys = labels + ids
    tile = 256

    def compare(k, best):
        if not own_pair:
            pltpu.make_async_copy(sources[0], held.at[k], sems.at[k]).wait()
        their_labels, their_ids = keys_of(held[k, ROWS:ROWS + EXTRA, :])
        label_column, id_column = column_of(their_labels), column_of(their_ids)
        place = where_ref[k]
        scores = [
            lax.dot_general(held[k, r:r + tile, :], held[0, 0:ROWS, :], (((1,), (1,)), ((), ())),
                            preferred_element_type=jnp.float32)
            for r in range(0, ROWS, tile)
        ]
        for index, r in enumerate(range(0, ROWS, tile)):
            low = jnp.concatenate([label_column[r:r + tile]] * (ROWS // 128), axis=1)
            own = jnp.concatenate([id_column[r:r + tile]] * (ROWS // 128), axis=1)
            gap = keys - low
            same = jnp.where((gap & -65536) == 0, scores[index], -1.0)
            earlier = gap < own
            for_rows = jnp.where(earlier, same, -1.0)
            halves = functools.reduce(jnp.maximum, [for_rows[:, c:c + 128] for c in range(0, ROWS, 128)])
            row_best = jnp.max(jnp.transpose(halves), axis=0, keepdims=True)
            old = table_ref[pl.ds(place, 1), r:r + tile]
            table_ref[pl.ds(place, 1), r:r + tile] = jnp.maximum(old, row_best)
            if not own_pair:
                for_columns = jnp.where(earlier, -1.0, same)
                best = jnp.maximum(best, jnp.max(for_columns.reshape(tile // 8, 8, ROWS), axis=0))
        return best

    first = 0 if own_pair else 1
    best = lax.fori_loop(first, first + count, compare, jnp.full((8, ROWS), -1.0, jnp.float32))
    if not own_pair:
        best = jnp.max(best, axis=0, keepdims=True)
        table_ref[block:block + 1, :] = jnp.maximum(table_ref[block:block + 1, :], best)


def stage(block, partners, blocks, table):
    own_pair = partners == (block,)
    sources = [blocks[block]] + ([] if own_pair else [blocks[p] for p in partners])
    where = jnp.array(([] if own_pair else [block]) + list(partners), jnp.int32)
    copies = len(sources)
    return pl.pallas_call(
        functools.partial(stage_kernel, block, partners),
        out_shape=jax.ShapeDtypeStruct((TABLE, ROWS), jnp.float32),
        in_specs=[pl.BlockSpec(memory_space=pl.ANY)] * copies
        + [pl.BlockSpec(memory_space=pltpu.SMEM), pl.BlockSpec(memory_space=pltpu.VMEM)],
        out_specs=pl.BlockSpec(memory_space=pltpu.VMEM),
        scratch_shapes=[
            pltpu.VMEM((copies, ROWS + EXTRA, FEATURES), jnp.bfloat16),
            pltpu.SemaphoreType.DMA((copies,)),
        ],
        compiler_params=pltpu.CompilerParams(vmem_limit_bytes=32 * MIB),
        cost_estimate=pl.CostEstimate(
            flops=2 * ROWS * ROWS * FEATURES * len(partners),
            bytes_accessed=copies * 2 * ROWS * FEATURES, transcendentals=0),
        name=f"compare_{block}",
    )(*sources, where, table)


def merge_kernel(table_ref, shared_ref, own_ref, *out_refs):
    merged = {i: jnp.maximum(table_ref[i:i + 1, :], shared_ref[n:n + 1, :]) for n, i in enumerate(SHARED)}
    for i in range(OWN):
        value = merged[i] if i in merged else table_ref[i:i + 1, :]
        (own_ref if i == 0 else out_refs[i - 1])[...] = value


def finish_kernel(rank_ref, *refs):
    out_ref = refs[-1]
    best = functools.reduce(jnp.maximum, [ref[...] for ref in refs[:-1]])
    column = jnp.concatenate([column_of(best)] * (ROWS // 128), axis=1)
    here = lax.broadcasted_iota(jnp.int32, (ROWS, ROWS), 0) == rank_ref[...]
    out_ref[...] = jnp.max(jnp.where(here, column, -2.0), axis=0, keepdims=True)


def per_device(embeddings, labels, row_ids):
    own, rank = prepare(embeddings, labels.reshape(1, ROWS), row_ids.reshape(1, ROWS))
    blocks = [own]
    for parent, axis, sign in EDGES:
        back = step_of(axis, -sign)
        blocks.append(lax.ppermute(blocks[parent], AXES, permutation(back)))
    for i in SHARED:
        blocks.append(lax.ppermute(blocks[i], AXES, permutation((0, 0, 0), swap=True)))
    table = jnp.full((TABLE, ROWS), -1.0, jnp.float32)
    for block, partners in STAGES:
        table = stage(block, partners, blocks, table)
    shared = lax.ppermute(table[OWN:BLOCKS], AXES, permutation((0, 0, 0), swap=True))
    vector = jax.ShapeDtypeStruct((1, ROWS), jnp.float32)
    found = pl.pallas_call(merge_kernel, out_shape=(vector,) * OWN, name="merge")(table, shared)
    returned = [found[0]]
    for value, offset in zip(found[1:], offsets()[1:]):
        returned.append(lax.ppermute(value, AXES, permutation(offset)))
    out = pl.pallas_call(finish_kernel, out_shape=vector, name="finish")(rank, *returned)
    return out.reshape(ROWS)


def solution(mesh):
    placed = (P(AXES, None), P(AXES, None), P(AXES))
    return jax.shard_map(
        per_device, mesh=mesh, in_specs=placed, out_specs=P(AXES), check_vma=False
    )
```

```python
import functools
import jax
import jax.numpy as jnp
from jax import lax
from jax.experimental import pallas as pl
from jax.experimental.pallas import tpu as pltpu
from jax.sharding import PartitionSpec as P

SIDE = 4
ROWS = 512
FEATURES = 1024
GROUPS = 8
CAPACITY = 96
HALF = CAPACITY // 2
EXTRA = 16
FIRST = HALF + EXTRA
PART = GROUPS * HALF
BLOCK = 2 * PART
MIB = 1 << 20
VMEM = pl.BlockSpec(memory_space=pltpu.VMEM)
ANY = pl.BlockSpec(memory_space=pl.ANY)
NT = (((1,), (1,)), ((), ()))


def column_of(row):
    return jnp.transpose(jnp.broadcast_to(row, (128, row.shape[1])))


def spread(row, lanes):
    return jnp.concatenate([column_of(row)] * (lanes // 128), axis=1)


def prepare_kernel(group_ref, emb_ref, label_ref, id_ref, first_ref, second_ref, place_ref):
    values = emb_ref[...]
    scale = lax.rsqrt(jnp.sum(values * values, axis=1, keepdims=True) + 1e-06)
    normed = (values * scale).astype(jnp.bfloat16)
    labels = label_ref[...]
    ids = id_ref[...]
    before = lax.broadcasted_iota(jnp.int32, (ROWS, ROWS), 0) < lax.broadcasted_iota(jnp.int32, (ROWS, ROWS), 1)
    alike = spread(labels, ROWS) == labels
    rank = jnp.sum((before & alike).astype(jnp.int32), axis=0, keepdims=True)
    in_first = rank < HALF
    within = jnp.where(in_first, rank, rank - HALF)
    to_first = jnp.where(in_first, labels * FIRST + rank, -1)
    to_second = jnp.where(in_first, -1, labels * HALF + within)

    def pick(target, count):
        return (lax.broadcasted_iota(jnp.int32, (count, ROWS), 0) == target).astype(jnp.bfloat16)

    def moved(target, count):
        return jnp.dot(pick(target, count), normed, preferred_element_type=jnp.float32).astype(jnp.bfloat16)

    first_ref[...] = moved(to_first, GROUPS * FIRST)
    second_ref[...] = moved(to_second, PART)
    place_ref[...] = jnp.where(in_first, 0, PART) + labels * HALF + within
    kind = lax.broadcasted_iota(jnp.int32, (8, ROWS), 0)
    digits = jnp.where(kind == 0, ids & 255, jnp.where(kind == 1, ids >> 8, jnp.where(kind == 2, 1, 0)))
    digits = jnp.concatenate([jnp.where(labels == c, digits, 0) for c in range(GROUPS)], axis=0)
    lane = jnp.where(in_first, 0, PART) + group_ref[0] * HALF + within
    digits = lax.dot_general(digits.astype(jnp.float32).astype(jnp.bfloat16), pick(lane, FEATURES), NT,
                             preferred_element_type=jnp.float32)
    for c in range(GROUPS):
        start = c * FIRST + HALF
        extra = jnp.concatenate([digits[8 * c:8 * c + 8], jnp.zeros((8, FEATURES), jnp.float32)], axis=0)
        first_ref[start:start + EXTRA, :] = extra.astype(jnp.bfloat16)


def prepare(embeddings, labels, row_ids, group):
    return pl.pallas_call(
        prepare_kernel,
        out_shape=(
            jax.ShapeDtypeStruct((GROUPS * FIRST, FEATURES), jnp.bfloat16),
            jax.ShapeDtypeStruct((PART, FEATURES), jnp.bfloat16),
            jax.ShapeDtypeStruct((1, ROWS), jnp.int32),
        ),
        in_specs=[pl.BlockSpec(memory_space=pltpu.SMEM)] + [VMEM] * 3,
        out_specs=(VMEM,) * 3,
        compiler_params=pltpu.CompilerParams(vmem_limit_bytes=32 * MIB),
        name="prepare",
    )(group, embeddings, labels, row_ids)


def gather_kernel(first_ref, out_ref):
    extra = jnp.zeros((EXTRA, FEATURES), jnp.float32)
    for s in range(GROUPS):
        out_ref[s * HALF:(s + 1) * HALF, :] = first_ref[s * FIRST:s * FIRST + HALF, :]
        extra = extra + first_ref[s * FIRST + HALF:(s + 1) * FIRST, :].astype(jnp.float32)
    out_ref[PART:PART + EXTRA, :] = extra.astype(jnp.bfloat16)


def gather_first(first):
    return pl.pallas_call(
        gather_kernel,
        out_shape=jax.ShapeDtypeStruct((PART + EXTRA, FEATURES), jnp.bfloat16),
        in_specs=[VMEM], out_specs=VMEM,
        compiler_params=pltpu.CompilerParams(vmem_limit_bytes=16 * MIB),
        name="gather_first",
    )(first)


def column_keys(extra):
    digits = extra[:, 0:BLOCK].astype(jnp.float32)
    return digits[0:1] + digits[1:2] * 256.0 + (1.0 - digits[2:3]) * 131072.0


def row_keys(extra):
    digit = lax.broadcasted_iota(jnp.int32, (EXTRA, 128), 0)
    weight = jnp.where(digit == 0, 1.0, jnp.where(digit == 1, 256.0, 0.0)).astype(jnp.bfloat16)
    return lax.dot_general(extra[:, 0:BLOCK], weight, (((0,), (0,)), ((), ())), preferred_element_type=jnp.float32)


def compare_kernel(products, names, *refs):
    count = len(names)
    sources = refs[:2 * count]
    before_ref, out_ref, held, extra, best, keys, sems = refs[2 * count:]
    copies = []
    for n in range(count):
        first, second = sources[2 * n], sources[2 * n + 1]
        copies.append((
            pltpu.make_async_copy(first.at[0:PART], held.at[n, 0:PART], sems.at[3 * n]),
            pltpu.make_async_copy(first.at[PART:PART + EXTRA], extra.at[n], sems.at[3 * n + 1]),
            pltpu.make_async_copy(second, held.at[n, PART:BLOCK], sems.at[3 * n + 2]),
        ))
        for copy in copies[-1]:
            copy.start()
    for group in copies:
        for copy in group:
            copy.wait()
    best[...] = jnp.full(best.shape, -1.0, jnp.float32)
    for n in range(count):
        keys[n] = row_keys(extra[n])

    def product(rows, columns):
        theirs = column_keys(extra[columns])
        for r in range(0, BLOCK, PART):
            scores = lax.dot_general(held[rows, r:r + PART, :], held[columns], NT, preferred_element_type=jnp.float32)
            own = jnp.concatenate([keys[rows, r:r + PART, :]] * (BLOCK // 128), axis=1)
            earlier = jnp.where(theirs < own, scores, -1.0)
            earlier = functools.reduce(jnp.maximum, [earlier[:, c:c + 128] for c in range(0, BLOCK, 128)])
            best[rows, r:r + PART, :] = jnp.maximum(best[rows, r:r + PART, :], earlier)

    for rows, columns in products:
        lax.fori_loop(0, len(rows) * len(columns), functools.partial(pair_step, product, rows, columns), 0)
    used = sorted({r for rows, _ in products for r in rows})
    out_ref[...] = before_ref[...]
    for r in used:
        found = jnp.max(jnp.transpose(best[r]), axis=0, keepdims=True)
        place = LINE.index(names[r])
        out_ref[place:place + 1, :] = jnp.maximum(out_ref[place:place + 1, :], found)


def pair_step(product, rows, columns, step, carry):
    product(rows[0] + lax.div(step, len(columns)), columns[0] + lax.rem(step, len(columns)))
    return carry


LINE = ("own", "xp", "xm", "xo")


def compare(names, products, blocks, best, name):
    count = len(names)
    operands = [part for n in names for part in blocks[n]]
    units = sum(len(r) * len(c) for r, c in products)
    return pl.pallas_call(
        functools.partial(compare_kernel, products, names),
        out_shape=jax.ShapeDtypeStruct((8, BLOCK), jnp.float32),
        in_specs=[ANY] * (2 * count) + [VMEM],
        out_specs=VMEM,
        scratch_shapes=[
            pltpu.VMEM((count, BLOCK, FEATURES), jnp.bfloat16),
            pltpu.VMEM((count, EXTRA, FEATURES), jnp.bfloat16),
            pltpu.VMEM((count, BLOCK, 128), jnp.float32),
            pltpu.VMEM((count, BLOCK, 128), jnp.float32),
            pltpu.SemaphoreType.DMA((3 * count,)),
        ],
        compiler_params=pltpu.CompilerParams(vmem_limit_bytes=40 * MIB),
        cost_estimate=pl.CostEstimate(flops=2 * units * BLOCK * BLOCK * FEATURES,
                                      bytes_accessed=count * 2 * BLOCK * FEATURES, transcendentals=0),
        name=name,
    )(*operands, best)


def finish_kernel(place_ref, value_ref, out_ref):
    here = lax.broadcasted_iota(jnp.int32, (BLOCK, ROWS), 0) == place_ref[...]
    out_ref[...] = jnp.max(jnp.where(here, spread(value_ref[...], ROWS), -2.0), axis=0, keepdims=True)


def move(value, dx, dy):
    pairs = [(y * SIDE + x, (y + dy) % SIDE * SIDE + (x + dx) % SIDE) for y in range(SIDE) for x in range(SIDE)]
    return lax.ppermute(value, "block", pairs)


def exchange(value):
    return lax.all_to_all(value, "group", split_axis=0, concat_axis=0, tiled=True)


def per_device(embeddings, labels, row_ids):
    group = lax.axis_index("group").astype(jnp.int32).reshape(1)
    first, second, place = prepare(embeddings, labels.reshape(1, ROWS), row_ids.reshape(1, ROWS), group)
    first = gather_first(exchange(first))
    second, first = lax.optimization_barrier((second, first))
    second = exchange(second)
    xp, xm, yp, ym = move(first, -1, 0), move(first, 1, 0), move(first, 0, -1), move(first, 0, 1)
    second, xp, xm, yp, ym = lax.optimization_barrier((second, xp, xm, yp, ym))
    xp2, xm2, yp2, ym2 = move(second, -1, 0), move(second, 1, 0), move(second, 0, -1), move(second, 0, 1)
    xo, yo = move(xp, -1, 0), move(yp, 0, -1)
    xo2, yo2 = move(xm2, 1, 0), move(ym2, 0, 1)
    blocks = dict(own=(first, second), xp=(xp, xp2), xm=(xm, xm2), yp=(yp, yp2), ym=(ym, ym2),
                  xo=(xo, xo2), yo=(yo, yo2))
    best = jnp.full((8, BLOCK), -1.0, jnp.float32)
    best = compare(("xp", "xm", "own", "yp", "ym"), (((0, 1, 2), (2, 3, 4)),), blocks, best, "compare_near")
    best = compare(("xo", "xp", "xm", "own", "yp", "ym", "yo"), (((0,), (3, 4, 5)), ((0, 1, 2, 3), (6,))),
                   blocks, best, "compare_far")
    own = best[0:1]
    for row, dx in ((1, 1), (2, -1), (3, 2)):
        own = jnp.maximum(own, move(best[row:row + 1], dx, 0))
    back = lax.all_to_all(own.reshape(2, GROUPS, HALF), "group", split_axis=1, concat_axis=1, tiled=True)
    out = pl.pallas_call(
        finish_kernel, out_shape=jax.ShapeDtypeStruct((1, ROWS), jnp.float32), name="finish",
    )(place, back.reshape(1, BLOCK))
    return out.reshape(ROWS)


def solution(mesh):
    placed = (P(("group", "block"), None), P(("group", "block"), None), P(("group", "block")))
    return jax.shard_map(
        per_device, mesh=mesh, in_specs=placed, out_specs=P(("group", "block")), check_vma=False
    )
```

```python
import functools
import jax
import jax.numpy as jnp
from jax import lax
from jax.experimental import pallas as pl
from jax.experimental.pallas import tpu as pltpu
from jax.sharding import PartitionSpec as P

SIDE = 4
CORES = 2
ROWS = 512
FEATURES = 1024
GROUPS = 8
CAPACITY = 96
EXTRA = 16
SENT = CAPACITY + EXTRA
JOINED = CORES * CAPACITY + EXTRA
BLOCK = GROUPS * CAPACITY
PART = BLOCK // 2
PIECES = 4
MIB = 1 << 20
AXES = ("group", "block")
SMEM = pl.BlockSpec(memory_space=pltpu.SMEM)
VMEM = pl.BlockSpec(memory_space=pltpu.VMEM)
NT = (((1,), (1,)), ((), ()))


def column_of(row):
    return jnp.transpose(jnp.broadcast_to(row, (128, row.shape[1])))


def spread(row, lanes):
    return jnp.concatenate([column_of(row)] * (lanes // 128), axis=1)


def prepare_kernel(where_ref, emb_ref, label_ref, id_ref, keep_ref, give_ref, place_ref,
                   values_ref, normed_ref, label_here, id_here, sems):
    step = ROWS // PIECES
    copies = [
        pltpu.make_async_copy(emb_ref.at[n * step:(n + 1) * step], values_ref.at[n * step:(n + 1) * step], sems.at[n])
        for n in range(PIECES)
    ]
    copies.append(pltpu.make_async_copy(label_ref, label_here, sems.at[PIECES]))
    copies.append(pltpu.make_async_copy(id_ref, id_here, sems.at[PIECES + 1]))
    for copy in copies[::-1]:
        copy.start()
    copies[PIECES].wait()
    copies[PIECES + 1].wait()
    labels = label_here[...]
    ids = id_here[...]
    core, x, z = where_ref[0], where_ref[1], where_ref[2]
    before = lax.broadcasted_iota(jnp.int32, (ROWS, ROWS), 0) < lax.broadcasted_iota(jnp.int32, (ROWS, ROWS), 1)
    alike = spread(labels, ROWS) == labels
    rank = jnp.sum((before & alike).astype(jnp.int32), axis=0, keepdims=True)
    plane = labels & (SIDE - 1)
    other = (labels >> 2) != core
    target = plane * SENT + rank

    def pick(target, count):
        return (lax.broadcasted_iota(jnp.int32, (count, ROWS), 0) == target).astype(jnp.bfloat16)

    slot = plane + jnp.where(other, SIDE, 0)
    place_ref[...] = slot * 128 + rank
    kind = lax.broadcasted_iota(jnp.int32, (8, ROWS), 0)
    digits = jnp.where(kind == 0, ids & 255, jnp.where(kind == 1, ids >> 8, jnp.where(kind == 2, 1, 0)))
    digits = jnp.concatenate([jnp.where(slot == n, digits, 0) for n in range(GROUPS)], axis=0)
    lane = jnp.where(labels < SIDE, z, x) * (CORES * CAPACITY) + jnp.where(other, CAPACITY, 0) + rank
    digits = lax.dot_general(digits.astype(jnp.float32).astype(jnp.bfloat16), pick(lane, FEATURES), NT,
                             preferred_element_type=jnp.float32)
    for n in range(PIECES):
        copies[n].wait()
        values = values_ref[n * step:(n + 1) * step, :]
        scale = lax.rsqrt(jnp.sum(values * values, axis=1, keepdims=True) + 1e-06)
        normed_ref[n * step:(n + 1) * step, :] = (values * scale).astype(jnp.bfloat16)
    for out_ref, chosen, first in ((give_ref, other, SIDE), (keep_ref, jnp.logical_not(other), 0)):
        moved = jnp.dot(pick(jnp.where(chosen, target, -1), SIDE * SENT), normed_ref[...],
                        preferred_element_type=jnp.float32)
        out_ref[...] = moved.astype(jnp.bfloat16)
        for n in range(SIDE):
            extra = jnp.concatenate(
                [digits[8 * (first + n):8 * (first + n) + 8], jnp.zeros((8, FEATURES), jnp.float32)], axis=0)
            out_ref[n * SENT + CAPACITY:(n + 1) * SENT, :] = extra.astype(jnp.bfloat16)


def prepare(where, embeddings, labels, row_ids):
    return pl.pallas_call(
        prepare_kernel,
        out_shape=(
            jax.ShapeDtypeStruct((SIDE * SENT, FEATURES), jnp.bfloat16),
            jax.ShapeDtypeStruct((SIDE * SENT, FEATURES), jnp.bfloat16),
            jax.ShapeDtypeStruct((1, ROWS), jnp.int32),
        ),
        in_specs=[SMEM] + [pl.BlockSpec(memory_space=pltpu.HBM)] * 3,
        out_specs=(VMEM,) * 3,
        scratch_shapes=[
            pltpu.VMEM((ROWS, FEATURES), jnp.float32),
            pltpu.VMEM((ROWS, FEATURES), jnp.bfloat16),
            pltpu.VMEM((1, ROWS), jnp.int32),
            pltpu.VMEM((1, ROWS), jnp.int32),
            pltpu.SemaphoreType.DMA((PIECES + 2,)),
        ],
        compiler_params=pltpu.CompilerParams(vmem_limit_bytes=60 * MIB),
        name="prepare",
    )(where, embeddings, labels, row_ids)


def join_kernel(keep_ref, got_ref, out_ref):
    for n in range(SIDE):
        for i, ref in enumerate((keep_ref, got_ref)):
            start = n * JOINED + i * CAPACITY
            out_ref[start:start + CAPACITY, :] = ref[n * SENT:n * SENT + CAPACITY, :]
        extra = [ref[n * SENT + CAPACITY:(n + 1) * SENT, :].astype(jnp.float32) for ref in (keep_ref, got_ref)]
        out_ref[(n + 1) * JOINED - EXTRA:(n + 1) * JOINED, :] = (extra[0] + extra[1]).astype(jnp.bfloat16)


def join(keep, got):
    return pl.pallas_call(
        join_kernel,
        out_shape=jax.ShapeDtypeStruct((SIDE * JOINED, FEATURES), jnp.bfloat16),
        in_specs=[VMEM] * 2, out_specs=VMEM,
        compiler_params=pltpu.CompilerParams(vmem_limit_bytes=16 * MIB),
        name="join",
    )(keep, got)


def gather_kernel(sent_ref, first_ref, second_ref):
    extra = jnp.zeros((EXTRA, FEATURES), jnp.float32)
    size = CORES * CAPACITY
    for n in range(SIDE):
        out_ref, start = (first_ref, second_ref)[n // 2], n % 2 * size
        out_ref[start:start + size, :] = sent_ref[n * JOINED:n * JOINED + size, :]
        extra = extra + sent_ref[n * JOINED + size:(n + 1) * JOINED, :].astype(jnp.float32)
    first_ref[PART:PART + EXTRA, :] = extra.astype(jnp.bfloat16)


def gather(sent):
    return pl.pallas_call(
        gather_kernel,
        out_shape=(jax.ShapeDtypeStruct((PART + EXTRA, FEATURES), jnp.bfloat16),
                   jax.ShapeDtypeStruct((PART, FEATURES), jnp.bfloat16)),
        in_specs=[VMEM], out_specs=(VMEM,) * 2,
        compiler_params=pltpu.CompilerParams(vmem_limit_bytes=16 * MIB),
        name="gather",
    )(sent)


def column_keys(extra):
    digits = extra[:, 0:BLOCK].astype(jnp.float32)
    return digits[0:1] + digits[1:2] * 256.0 + (1.0 - digits[2:3]) * 131072.0


def row_keys(extra):
    digit = lax.broadcasted_iota(jnp.int32, (EXTRA, 128), 0)
    weight = jnp.where(digit == 0, 1.0, jnp.where(digit == 1, 256.0, jnp.where(digit == 2, -131072.0, 0.0)))
    keys = lax.dot_general(extra[:, 0:BLOCK], weight.astype(jnp.bfloat16), (((0,), (0,)), ((), ())),
                           preferred_element_type=jnp.float32)
    return keys + 131072.0


def lane_tiles(values):
    return functools.reduce(jnp.maximum, [values[:, n:n + 128] for n in range(0, BLOCK, 128)])


def halves(refs, n):
    return (refs[2 * n][0:PART, :], 0), (refs[2 * n + 1][...], PART)


def scores_of(left, right):
    return lax.dot_general(left, right, NT, preferred_element_type=jnp.float32)


class Whole:
    def __init__(self, refs, wanted, held, sems):
        self.copies = []
        for i, n in enumerate(wanted):
            self.copies.append(pltpu.make_async_copy(refs[2 * n].at[0:PART], held.at[i, 0:PART], sems.at[2 * i]))
            self.copies.append(pltpu.make_async_copy(refs[2 * n + 1], held.at[i, PART:BLOCK], sems.at[2 * i + 1]))
        for copy in self.copies:
            copy.start()

    def wait(self, i):
        self.copies[2 * i].wait()
        self.copies[2 * i + 1].wait()


NAMES = ("own", "up", "um", "uo", "yp", "yo")


def by_group(row):
    empty = jnp.zeros((1, 128 - CAPACITY), jnp.float32)
    return jnp.concatenate(
        [jnp.concatenate([row[:, n * CAPACITY:(n + 1) * CAPACITY], empty], axis=1) for n in range(GROUPS)], axis=0)


def compare_kernel(names, products, last, before_ref, *refs):
    sources, refs = refs[:2 * len(names)], refs[2 * len(names):]
    out_refs, (held, sems) = refs[:-2], refs[-2:]
    whole = Whole(sources, [names.index(columns) for columns, _ in products], held, sems)
    extras = [sources[2 * n][PART:PART + EXTRA, :] for n in range(len(names))]
    found = {}

    def note(name, values):
        found[name] = jnp.maximum(found[name], values) if name in found else values

    for i, (columns, uses) in enumerate(products):
        theirs = column_keys(extras[names.index(columns)])
        columns_best = jnp.full((8, BLOCK), -1.0, jnp.float32)
        whole.wait(i)
        for rows, for_rows, for_columns in uses:
            n = names.index(rows)
            keys = row_keys(extras[n])
            rows_best = []
            for part, r in halves(sources, n):
                own = jnp.concatenate([keys[r:r + PART, :]] * (BLOCK // 128), axis=1)
                scores = scores_of(part, held[i])
                earlier = theirs < own
                if for_rows:
                    rows_best.append(lane_tiles(jnp.where(earlier, scores, -1.0)))
                if for_columns:
                    later = jnp.where(earlier, -1.0, scores)
                    columns_best = jnp.maximum(columns_best, jnp.max(later.reshape(PART // 8, 8, BLOCK), axis=0))
            if for_rows:
                note(rows, jnp.max(jnp.transpose(jnp.concatenate(rows_best, axis=0)), axis=0, keepdims=True))
        if any(use[2] for use in uses):
            note(columns, jnp.max(columns_best, axis=0, keepdims=True))
    for n, name in enumerate(NAMES):
        values = before_ref[n:n + 1, :]
        if name in found:
            values = jnp.maximum(values, found[name])
        if last:
            out_refs[n][...] = by_group(values)
        else:
            out_refs[0][n:n + 1, :] = values


def compare(blocks, before, products, name, last=False):
    names = []
    for columns, uses in products:
        for block in [columns] + [use[0] for use in uses]:
            if block not in names:
                names.append(block)
    units = sum(len(uses) for _, uses in products)
    shape = jax.ShapeDtypeStruct((GROUPS, 128), jnp.float32)
    return pl.pallas_call(
        functools.partial(compare_kernel, names, products, last),
        out_shape=(shape,) * len(NAMES) if last else jax.ShapeDtypeStruct((8, BLOCK), jnp.float32),
        in_specs=[VMEM] * (1 + 2 * len(names)),
        out_specs=(VMEM,) * len(NAMES) if last else VMEM,
        scratch_shapes=[
            pltpu.VMEM((len(products), BLOCK, FEATURES), jnp.bfloat16),
            pltpu.SemaphoreType.DMA((2 * len(products),)),
        ],
        compiler_params=pltpu.CompilerParams(vmem_limit_bytes=36 * MIB),
        cost_estimate=pl.CostEstimate(flops=2 * units * BLOCK * BLOCK * FEATURES,
                                      bytes_accessed=2 * BLOCK * FEATURES, transcendentals=0),
        name=name,
    )(before, *[part for block in names for part in blocks[block]])


def finish_kernel(place_ref, kept_ref, got_ref, out_ref):
    rows = [kept_ref[CORES * n:CORES * n + 1, :] for n in range(SIDE)]
    rows = rows + [got_ref[CORES * n + 1:CORES * n + 2, :] for n in range(SIDE)]
    columns = jnp.transpose(jnp.concatenate(rows + [jnp.zeros((128 - GROUPS, 128), jnp.float32)], axis=0))
    best = jnp.full((128, ROWS), -2.0, jnp.float32)
    here = lax.broadcasted_iota(jnp.int32, (128, ROWS), 0)
    for n in range(GROUPS):
        best = jnp.where(here == place_ref[...] - 128 * n, columns[:, n:n + 1], best)
    out_ref[...] = jnp.max(best, axis=0, keepdims=True)


def device_at(x, y, z, core):
    return (z * CORES + core) * SIDE * SIDE + y * SIDE + x


def everywhere():
    return [(x, y, z, core) for z in range(SIDE) for core in range(CORES) for y in range(SIDE) for x in range(SIDE)]


def move(value, along, up):
    pairs = []
    for x, y, z, core in everywhere():
        dx, dy, dz = (0, -up, along) if core else (along, up, 0)
        pairs.append((device_at(x, y, z, core), device_at((x + dx) % SIDE, (y + dy) % SIDE, (z + dz) % SIDE, core)))
    return lax.ppermute(value, AXES, pairs)


def swap(value):
    pairs = [(device_at(x, y, z, core), device_at(x, y, z, 1 - core)) for x, y, z, core in everywhere()]
    return lax.ppermute(value, AXES, pairs)


def exchange(value):
    span = range(SIDE)
    lines = [[device_at(x, y, z, 0) for z in span] for x in span for y in span]
    lines = lines + [[device_at(x, y, z, 1) for x in span] for z in span for y in span]
    return lax.all_to_all(value, AXES, split_axis=0, concat_axis=0, tiled=True, axis_index_groups=lines)


def per_device(embeddings, labels, row_ids):
    group, block = lax.axis_index("group"), lax.axis_index("block")
    where = jnp.stack([group % CORES, block % SIDE, group // CORES]).astype(jnp.int32)
    keep, give, place = prepare(where, embeddings, labels.reshape(1, ROWS), row_ids.reshape(1, ROWS))
    own = gather(exchange(join(keep, swap(give))))
    yp = [move(part, 0, -1) for part in own]
    up = [move(part, -1, 0) for part in own]
    um = [move(part, 1, 0) for part in own]
    yo = [move(part, 0, -1) for part in yp]
    uo = [move(up[0], -1, 0), move(um[1], 1, 0)]
    blocks = dict(own=own, up=up, um=um, uo=uo, yp=yp, yo=yo)
    best = jnp.full((8, BLOCK), -1.0, jnp.float32)
    best = compare(blocks, best, (
        ("own", (("own", True, False), ("up", True, True))),
        ("yp", (("own", True, True), ("up", True, True), ("um", True, True))),
    ), "compare_near")
    best = compare(blocks, best, (
        ("own", (("uo", False, True),)),
        ("yp", (("uo", True, True),)),
    ), "compare_line")
    best = compare(blocks, best, (
        ("yo", (("own", True, False), ("up", True, True), ("uo", True, False))),
    ), "compare_far", last=True)
    found = best[0]
    for value, along, up in zip(best[1:], (1, -1, 2, 0, 0), (0, 0, 0, 1, 2)):
        found = jnp.maximum(found, move(value, along, up))
    kept = exchange(found)
    out = pl.pallas_call(
        finish_kernel, out_shape=jax.ShapeDtypeStruct((1, ROWS), jnp.float32), name="finish",
    )(place, kept, swap(kept))
    return out.reshape(ROWS)


def solution(mesh):
    placed = (P(AXES, None), P(AXES, None), P(AXES))
    return jax.shard_map(
        per_device, mesh=mesh, in_specs=placed, out_specs=P(AXES), check_vma=False
    )
```

```python
import functools
import jax
import jax.numpy as jnp
from jax import lax
from jax.experimental import pallas as pl
from jax.experimental.pallas import tpu as pltpu
from jax.sharding import PartitionSpec as P

SIDE = 4
CORES = 2
ROWS = 512
FEATURES = 1024
GROUPS = 8
CAPACITY = 96
EXTRA = 16
SENT = CAPACITY + EXTRA
JOINED = CORES * CAPACITY + EXTRA
BLOCK = GROUPS * CAPACITY
PART = BLOCK // 2
FIRST = PART + EXTRA
PIECES = 4
MIB = 1 << 20
AXES = ("group", "block")
VMEM = pl.BlockSpec(memory_space=pltpu.VMEM)
NT = (((1,), (1,)), ((), ()))


def column_of(row):
    return jnp.transpose(jnp.broadcast_to(row, (128, row.shape[1])))


def spread(row, lanes):
    return jnp.concatenate([column_of(row)] * (lanes // 128), axis=1)


def prepare_kernel(emb_ref, label_ref, id_ref, keep_ref, give_ref, place_ref,
                   values_ref, normed_ref, label_here, id_here, sems):
    step = ROWS // PIECES
    copies = [
        pltpu.make_async_copy(emb_ref.at[n * step:(n + 1) * step], values_ref.at[n * step:(n + 1) * step], sems.at[n])
        for n in range(PIECES)
    ]
    copies.append(pltpu.make_async_copy(label_ref, label_here, sems.at[PIECES]))
    copies.append(pltpu.make_async_copy(id_ref, id_here, sems.at[PIECES + 1]))
    for copy in copies[::-1]:
        copy.start()
    copies[PIECES].wait()
    copies[PIECES + 1].wait()
    labels = label_here[...]
    ids = id_here[...]
    group = lax.axis_index("group")
    core, x, z = group & 1, lax.axis_index("block") & (SIDE - 1), group >> 1
    before = lax.broadcasted_iota(jnp.int32, (ROWS, ROWS), 0) < lax.broadcasted_iota(jnp.int32, (ROWS, ROWS), 1)
    alike = spread(labels, ROWS) == labels
    rank = jnp.sum((before & alike).astype(jnp.int32), axis=0, keepdims=True)
    plane = labels & (SIDE - 1)
    other = (labels >> 2) != core
    target = plane * SENT + rank

    def pick(target, count):
        return (lax.broadcasted_iota(jnp.int32, (count, ROWS), 0) == target).astype(jnp.bfloat16)

    slot = plane + jnp.where(other, SIDE, 0)
    place_ref[...] = slot * 128 + rank
    kind = lax.broadcasted_iota(jnp.int32, (8, ROWS), 0)
    digits = jnp.where(kind == 0, ids & 255, jnp.where(kind == 1, ids >> 8, jnp.where(kind == 2, 1, 0)))
    digits = jnp.concatenate([jnp.where(slot == n, digits, 0) for n in range(GROUPS)], axis=0)
    lane = jnp.where(labels < SIDE, z, x) * (CORES * CAPACITY) + jnp.where(other, CAPACITY, 0) + rank
    digits = lax.dot_general(digits.astype(jnp.float32).astype(jnp.bfloat16), pick(lane, FEATURES), NT,
                             preferred_element_type=jnp.float32)
    for n in range(PIECES):
        copies[n].wait()
        values = values_ref[n * step:(n + 1) * step, :]
        scale = lax.rsqrt(jnp.sum(values * values, axis=1, keepdims=True) + 1e-06)
        normed_ref[n * step:(n + 1) * step, :] = (values * scale).astype(jnp.bfloat16)
    for out_ref, chosen, first in ((give_ref, other, SIDE), (keep_ref, jnp.logical_not(other), 0)):
        moved = jnp.dot(pick(jnp.where(chosen, target, -1), SIDE * SENT), normed_ref[...],
                        preferred_element_type=jnp.float32)
        out_ref[...] = moved.astype(jnp.bfloat16)
        for n in range(SIDE):
            extra = jnp.concatenate(
                [digits[8 * (first + n):8 * (first + n) + 8], jnp.zeros((8, FEATURES), jnp.float32)], axis=0)
            out_ref[n * SENT + CAPACITY:(n + 1) * SENT, :] = extra.astype(jnp.bfloat16)


def prepare(embeddings, labels, row_ids):
    return pl.pallas_call(
        prepare_kernel,
        out_shape=(
            jax.ShapeDtypeStruct((SIDE * SENT, FEATURES), jnp.bfloat16),
            jax.ShapeDtypeStruct((SIDE * SENT, FEATURES), jnp.bfloat16),
            jax.ShapeDtypeStruct((1, ROWS), jnp.int32),
        ),
        in_specs=[pl.BlockSpec(memory_space=pltpu.HBM)] * 3,
        out_specs=(VMEM,) * 3,
        scratch_shapes=[
            pltpu.VMEM((ROWS, FEATURES), jnp.float32),
            pltpu.VMEM((ROWS, FEATURES), jnp.bfloat16),
            pltpu.VMEM((1, ROWS), jnp.int32),
            pltpu.VMEM((1, ROWS), jnp.int32),
            pltpu.SemaphoreType.DMA((PIECES + 2,)),
        ],
        compiler_params=pltpu.CompilerParams(vmem_limit_bytes=60 * MIB),
        name="prepare",
    )(embeddings, labels, row_ids)


def plane():
    group = lax.axis_index("group")
    return jnp.where((group & 1) == 1, lax.axis_index("block") & (SIDE - 1), group >> 1)


def join_kernel(keep_ref, got_ref, *out_refs):
    for n in range(SIDE):
        start = ((plane() + n) & (SIDE - 1)) * SENT
        extra = jnp.zeros((EXTRA, FEATURES), jnp.float32)
        for i, ref in enumerate((keep_ref, got_ref)):
            rows = ref[pl.ds(pl.multiple_of(start, 16), CAPACITY), :]
            out_refs[n][i * CAPACITY:(i + 1) * CAPACITY, :] = rows
            extra = extra + ref[pl.ds(pl.multiple_of(start + CAPACITY, 16), EXTRA), :].astype(jnp.float32)
        out_refs[n][JOINED - EXTRA:JOINED, :] = extra.astype(jnp.bfloat16)


def join(keep, got):
    return pl.pallas_call(
        join_kernel,
        out_shape=(jax.ShapeDtypeStruct((JOINED, FEATURES), jnp.bfloat16),) * SIDE,
        in_specs=[VMEM] * 2, out_specs=(VMEM,) * SIDE,
        compiler_params=pltpu.CompilerParams(vmem_limit_bytes=16 * MIB),
        name="join",
    )(keep, got)


def gather_kernel(*refs):
    out_ref = refs[SIDE]
    extra = jnp.zeros((EXTRA, FEATURES), jnp.float32)
    size = CORES * CAPACITY
    for n in range(SIDE):
        source = (plane() - n) & (SIDE - 1)
        start = source * size + (source >> 1) * EXTRA
        out_ref[pl.ds(pl.multiple_of(start, 16), size), :] = refs[n][0:size, :]
        extra = extra + refs[n][size:JOINED, :].astype(jnp.float32)
    out_ref[PART:FIRST, :] = extra.astype(jnp.bfloat16)


def gather(pieces):
    return pl.pallas_call(
        gather_kernel,
        out_shape=jax.ShapeDtypeStruct((BLOCK + EXTRA, FEATURES), jnp.bfloat16),
        in_specs=[VMEM] * SIDE, out_specs=VMEM,
        compiler_params=pltpu.CompilerParams(vmem_limit_bytes=16 * MIB),
        name="gather",
    )(*pieces)


def column_keys(extra):
    digits = extra[:, 0:BLOCK].astype(jnp.float32)
    return digits[0:1] + digits[1:2] * 256.0 + (1.0 - digits[2:3]) * 131072.0


def row_keys(extra):
    digit = lax.broadcasted_iota(jnp.int32, (EXTRA, 128), 0)
    weight = jnp.where(digit == 0, 1.0, jnp.where(digit == 1, 256.0, jnp.where(digit == 2, -131072.0, 0.0)))
    keys = lax.dot_general(extra[:, 0:BLOCK], weight.astype(jnp.bfloat16), (((0,), (0,)), ((), ())),
                           preferred_element_type=jnp.float32)
    return keys + 131072.0


def lane_tiles(values):
    return functools.reduce(jnp.maximum, [values[:, n:n + 128] for n in range(0, BLOCK, 128)])


def halves(refs):
    if len(refs) == 1:
        return refs[0].at[0:PART], refs[0].at[FIRST:FIRST + PART]
    return refs[0].at[0:PART], refs[1]


def scores_of(left, right):
    return lax.dot_general(left, right, NT, preferred_element_type=jnp.float32)


class Whole:
    def __init__(self, wanted, held, sems):
        self.copies = []
        for i, refs in enumerate(wanted):
            for n, part in enumerate(halves(refs)):
                self.copies.append(
                    pltpu.make_async_copy(part, held.at[i, n * PART:(n + 1) * PART], sems.at[2 * i + n]))
        for copy in self.copies:
            copy.start()

    def wait(self, i):
        self.copies[2 * i].wait()
        self.copies[2 * i + 1].wait()


NAMES = ("own", "up", "um", "uo", "yp", "yo")


def by_group(row):
    empty = jnp.zeros((1, 128 - CAPACITY), jnp.float32)
    return jnp.concatenate(
        [jnp.concatenate([row[:, n * CAPACITY:(n + 1) * CAPACITY], empty], axis=1) for n in range(GROUPS)], axis=0)


def compare_kernel(sizes, products, ready, before_ref, *refs):
    sources = {}
    for block, size in sizes:
        sources[block], refs = refs[:size], refs[size:]
    out_refs, (held, sems) = refs[:-2], refs[-2:]
    whole = Whole([sources[columns] for columns, _ in products], held, sems)
    extras = {block: refs_of[0][PART:FIRST, :] for block, refs_of in sources.items()}
    found = {}

    def note(name, values):
        found[name] = jnp.maximum(found[name], values) if name in found else values

    for i, (columns, uses) in enumerate(products):
        theirs = column_keys(extras[columns])
        columns_best = jnp.full((8, BLOCK), -1.0, jnp.float32)
        whole.wait(i)
        for rows, for_rows, for_columns in uses:
            keys = row_keys(extras[rows])
            rows_best = []
            for part, r in zip(halves(sources[rows]), (0, PART)):
                own = jnp.concatenate([keys[r:r + PART, :]] * (BLOCK // 128), axis=1)
                scores = scores_of(part[...], held[i])
                earlier = theirs < own
                if for_rows:
                    rows_best.append(lane_tiles(jnp.where(earlier, scores, -1.0)))
                if for_columns:
                    later = jnp.where(earlier, -1.0, scores)
                    columns_best = jnp.maximum(columns_best, jnp.max(later.reshape(PART // 8, 8, BLOCK), axis=0))
            if for_rows:
                note(rows, jnp.max(jnp.transpose(jnp.concatenate(rows_best, axis=0)), axis=0, keepdims=True))
        if any(use[2] for use in uses):
            note(columns, jnp.max(columns_best, axis=0, keepdims=True))
    for n, name in enumerate(NAMES):
        values = before_ref[n:n + 1, :]
        if name in found:
            values = jnp.maximum(values, found[name])
        if name in ready:
            out_refs[1 + ready.index(name)][...] = by_group(values)
        out_refs[0][n:n + 1, :] = values


def compare(blocks, before, products, name, ready=()):
    names = []
    for columns, uses in products:
        for block in [columns] + [use[0] for use in uses]:
            if block not in names:
                names.append(block)
    units = sum(len(uses) for _, uses in products)
    shape = jax.ShapeDtypeStruct((GROUPS, 128), jnp.float32)
    return pl.pallas_call(
        functools.partial(compare_kernel, [(block, len(blocks[block])) for block in names], products, ready),
        out_shape=(jax.ShapeDtypeStruct((8, BLOCK), jnp.float32),) + (shape,) * len(ready),
        in_specs=[VMEM] * (1 + sum(len(blocks[block]) for block in names)),
        out_specs=(VMEM,) * (1 + len(ready)),
        scratch_shapes=[
            pltpu.VMEM((len(products), BLOCK, FEATURES), jnp.bfloat16),
            pltpu.SemaphoreType.DMA((2 * len(products),)),
        ],
        compiler_params=pltpu.CompilerParams(vmem_limit_bytes=36 * MIB),
        cost_estimate=pl.CostEstimate(flops=2 * units * BLOCK * BLOCK * FEATURES,
                                      bytes_accessed=2 * BLOCK * FEATURES, transcendentals=0),
        name=name,
    )(before, *[part for block in names for part in blocks[block]])


def finish_kernel(place_ref, kept_ref, got_ref, out_ref):
    rows = [kept_ref[CORES * n:CORES * n + 1, :] for n in range(SIDE)]
    rows = rows + [got_ref[CORES * n + 1:CORES * n + 2, :] for n in range(SIDE)]
    columns = jnp.transpose(jnp.concatenate(rows + [jnp.zeros((128 - GROUPS, 128), jnp.float32)], axis=0))
    best = jnp.full((128, ROWS), -2.0, jnp.float32)
    here = lax.broadcasted_iota(jnp.int32, (128, ROWS), 0)
    for n in range(GROUPS):
        best = jnp.where(here == place_ref[...] - 128 * n, columns[:, n:n + 1], best)
    out_ref[...] = jnp.max(best, axis=0, keepdims=True)


def device_at(x, y, z, core):
    return (z * CORES + core) * SIDE * SIDE + y * SIDE + x


def everywhere():
    return [(x, y, z, core) for z in range(SIDE) for core in range(CORES) for y in range(SIDE) for x in range(SIDE)]


def move(value, along, up):
    pairs = []
    for x, y, z, core in everywhere():
        dx, dy, dz = (0, -up, along) if core else (along, up, 0)
        pairs.append((device_at(x, y, z, core), device_at((x + dx) % SIDE, (y + dy) % SIDE, (z + dz) % SIDE, core)))
    return lax.ppermute(value, AXES, pairs)


def swap(value):
    pairs = [(device_at(x, y, z, core), device_at(x, y, z, 1 - core)) for x, y, z, core in everywhere()]
    return lax.ppermute(value, AXES, pairs)


def climb(value, planes):
    pairs = []
    for x, y, z, core in everywhere():
        dx, dz = (planes, 0) if core else (0, planes)
        pairs.append((device_at(x, y, z, core), device_at((x + dx) % SIDE, y, (z + dz) % SIDE, core)))
    return lax.ppermute(value, AXES, pairs)


def exchange(value):
    span = range(SIDE)
    lines = [[device_at(x, y, z, 0) for z in span] for x in span for y in span]
    lines = lines + [[device_at(x, y, z, 1) for x in span] for z in span for y in span]
    return lax.all_to_all(value, AXES, split_axis=0, concat_axis=0, tiled=True, axis_index_groups=lines)


def per_device(embeddings, labels, row_ids):
    keep, give, place = prepare(embeddings, labels.reshape(1, ROWS), row_ids.reshape(1, ROWS))
    pieces = join(keep, swap(give))
    own = gather([climb(piece, n) if n else piece for n, piece in enumerate(pieces)])
    yp, up, um = move(own, 0, -1), move(own, -1, 0), move(own, 1, 0)
    yp, up, um = lax.optimization_barrier((yp, up, um))
    yo = move(yp, 0, -1)
    uo = move(up[0:FIRST], -1, 0), move(um[FIRST:FIRST + PART], 1, 0)
    blocks = dict(own=(own,), up=(up,), um=(um,), uo=uo, yp=(yp,), yo=(yo,))
    best = jnp.full((8, BLOCK), -1.0, jnp.float32)
    best, = compare(blocks, best, (
        ("own", (("own", True, False), ("up", True, True))),
        ("yp", (("own", True, True), ("up", True, True), ("um", True, True))),
    ), "compare_near")
    best, for_um, for_uo, for_yp = compare(blocks, best, (
        ("own", (("uo", False, True),)),
        ("yp", (("uo", True, True),)),
    ), "compare_line", ("um", "uo", "yp"))
    back = [move(for_um, -1, 0), move(for_uo, 2, 0), move(for_yp, 0, 1)]
    best, found, for_up, for_yo = compare(blocks, best, (
        ("yo", (("own", True, False), ("up", True, True), ("uo", False, True))),
    ), "compare_far", ("own", "up", "yo"))
    for_up, for_yo, *back = lax.optimization_barrier((for_up, for_yo, *back))
    back = back + [move(for_up, 1, 0), move(for_yo, 0, 2)]
    found = functools.reduce(jnp.maximum, back, found)
    kept = exchange(found)
    out = pl.pallas_call(
        finish_kernel, out_shape=jax.ShapeDtypeStruct((1, ROWS), jnp.float32), name="finish",
    )(place, kept, swap(kept))
    return out.reshape(ROWS)


def solution(mesh):
    placed = (P(AXES, None), P(AXES, None), P(AXES))
    return jax.shard_map(
        per_device, mesh=mesh, in_specs=placed, out_specs=P(AXES), check_vma=False
    )
```

```python
import functools
import jax
import jax.numpy as jnp
from jax import lax
from jax.experimental import pallas as pl
from jax.experimental.pallas import tpu as pltpu
from jax.sharding import PartitionSpec as P

SIDE = 4
CORES = 2
ROWS = 512
FEATURES = 1024
GROUPS = 8
CAPACITY = 96
EXTRA = 16
SENT = CAPACITY + EXTRA
JOINED = CORES * CAPACITY + EXTRA
BLOCK = GROUPS * CAPACITY
PART = BLOCK // 2
FIRST = PART + EXTRA
PIECES = 4
MIB = 1 << 20
AXES = ("group", "block")
VMEM = pl.BlockSpec(memory_space=pltpu.VMEM)
NT = (((1,), (1,)), ((), ()))


def column_of(row):
    return jnp.transpose(jnp.broadcast_to(row, (128, row.shape[1])))


def spread(row, lanes):
    return jnp.concatenate([column_of(row)] * (lanes // 128), axis=1)


def prepare_kernel(emb_ref, label_ref, id_ref, keep_ref, give_ref, place_ref,
                   values_ref, normed_ref, label_here, id_here, sems):
    step = ROWS // PIECES
    copies = [
        pltpu.make_async_copy(emb_ref.at[n * step:(n + 1) * step], values_ref.at[n * step:(n + 1) * step], sems.at[n])
        for n in range(PIECES)
    ]
    copies.append(pltpu.make_async_copy(label_ref, label_here, sems.at[PIECES]))
    copies.append(pltpu.make_async_copy(id_ref, id_here, sems.at[PIECES + 1]))
    for copy in copies[::-1]:
        copy.start()
    copies[PIECES].wait()
    copies[PIECES + 1].wait()
    labels = label_here[...]
    ids = id_here[...]
    group = lax.axis_index("group")
    core, x, z = group & 1, lax.axis_index("block") & (SIDE - 1), group >> 1
    before = lax.broadcasted_iota(jnp.int32, (ROWS, ROWS), 0) < lax.broadcasted_iota(jnp.int32, (ROWS, ROWS), 1)
    alike = spread(labels, ROWS) == labels
    rank = jnp.sum((before & alike).astype(jnp.int32), axis=0, keepdims=True)
    plane = labels & (SIDE - 1)
    other = (labels >> 2) != core
    target = plane * SENT + rank

    def pick(target, count):
        return (lax.broadcasted_iota(jnp.int32, (count, ROWS), 0) == target).astype(jnp.bfloat16)

    slot = plane + jnp.where(other, SIDE, 0)
    place_ref[...] = slot * 128 + rank
    kind = lax.broadcasted_iota(jnp.int32, (8, ROWS), 0)
    digits = jnp.where(kind == 0, ids & 255, jnp.where(kind == 1, ids >> 8, jnp.where(kind == 2, 1, 0)))
    digits = jnp.concatenate([jnp.where(slot == n, digits, 0) for n in range(GROUPS)], axis=0)
    lane = jnp.where(labels < SIDE, z, x) * (CORES * CAPACITY) + jnp.where(other, CAPACITY, 0) + rank
    digits = lax.dot_general(digits.astype(jnp.float32).astype(jnp.bfloat16), pick(lane, FEATURES), NT,
                             preferred_element_type=jnp.float32)
    for n in range(PIECES):
        copies[n].wait()
        values = values_ref[n * step:(n + 1) * step, :]
        scale = lax.rsqrt(jnp.sum(values * values, axis=1, keepdims=True) + 1e-06)
        normed_ref[n * step:(n + 1) * step, :] = (values * scale).astype(jnp.bfloat16)
    for out_ref, chosen, first in ((give_ref, other, SIDE), (keep_ref, jnp.logical_not(other), 0)):
        moved = jnp.dot(pick(jnp.where(chosen, target, -1), SIDE * SENT), normed_ref[...],
                        preferred_element_type=jnp.float32)
        out_ref[...] = moved.astype(jnp.bfloat16)
        for n in range(SIDE):
            extra = jnp.concatenate(
                [digits[8 * (first + n):8 * (first + n) + 8], jnp.zeros((8, FEATURES), jnp.float32)], axis=0)
            out_ref[n * SENT + CAPACITY:(n + 1) * SENT, :] = extra.astype(jnp.bfloat16)


def prepare(embeddings, labels, row_ids):
    return pl.pallas_call(
        prepare_kernel,
        out_shape=(
            jax.ShapeDtypeStruct((SIDE * SENT, FEATURES), jnp.bfloat16),
            jax.ShapeDtypeStruct((SIDE * SENT, FEATURES), jnp.bfloat16),
            jax.ShapeDtypeStruct((1, ROWS), jnp.int32),
        ),
        in_specs=[pl.BlockSpec(memory_space=pltpu.HBM)] * 3,
        out_specs=(VMEM,) * 3,
        scratch_shapes=[
            pltpu.VMEM((ROWS, FEATURES), jnp.float32),
            pltpu.VMEM((ROWS, FEATURES), jnp.bfloat16),
            pltpu.VMEM((1, ROWS), jnp.int32),
            pltpu.VMEM((1, ROWS), jnp.int32),
            pltpu.SemaphoreType.DMA((PIECES + 2,)),
        ],
        compiler_params=pltpu.CompilerParams(vmem_limit_bytes=60 * MIB),
        name="prepare",
    )(embeddings, labels, row_ids)


def plane():
    group = lax.axis_index("group")
    return jnp.where((group & 1) == 1, lax.axis_index("block") & (SIDE - 1), group >> 1)


def join_kernel(keep_ref, got_ref, *out_refs):
    for n in range(SIDE):
        start = ((plane() + n) & (SIDE - 1)) * SENT
        extra = jnp.zeros((EXTRA, FEATURES), jnp.float32)
        for i, ref in enumerate((keep_ref, got_ref)):
            rows = ref[pl.ds(pl.multiple_of(start, 16), CAPACITY), :]
            out_refs[n][i * CAPACITY:(i + 1) * CAPACITY, :] = rows
            extra = extra + ref[pl.ds(pl.multiple_of(start + CAPACITY, 16), EXTRA), :].astype(jnp.float32)
        out_refs[n][JOINED - EXTRA:JOINED, :] = extra.astype(jnp.bfloat16)


def join(keep, got):
    return pl.pallas_call(
        join_kernel,
        out_shape=(jax.ShapeDtypeStruct((JOINED, FEATURES), jnp.bfloat16),) * SIDE,
        in_specs=[VMEM] * 2, out_specs=(VMEM,) * SIDE,
        compiler_params=pltpu.CompilerParams(vmem_limit_bytes=16 * MIB),
        name="join",
    )(keep, got)


def gather_kernel(*refs):
    out_ref = refs[SIDE]
    extra = jnp.zeros((EXTRA, FEATURES), jnp.float32)
    size = CORES * CAPACITY
    for n in range(SIDE):
        source = (plane() - n) & (SIDE - 1)
        start = source * size + (source >> 1) * EXTRA
        out_ref[pl.ds(pl.multiple_of(start, 16), size), :] = refs[n][0:size, :]
        extra = extra + refs[n][size:JOINED, :].astype(jnp.float32)
    out_ref[PART:FIRST, :] = extra.astype(jnp.bfloat16)


def gather(pieces):
    return pl.pallas_call(
        gather_kernel,
        out_shape=jax.ShapeDtypeStruct((BLOCK + EXTRA, FEATURES), jnp.bfloat16),
        in_specs=[VMEM] * SIDE, out_specs=VMEM,
        compiler_params=pltpu.CompilerParams(vmem_limit_bytes=16 * MIB),
        name="gather",
    )(*pieces)


def column_keys(extra):
    digits = extra[:, 0:BLOCK].astype(jnp.float32)
    return digits[0:1] + digits[1:2] * 256.0 + (1.0 - digits[2:3]) * 131072.0


def row_keys(extra):
    digit = lax.broadcasted_iota(jnp.int32, (EXTRA, 128), 0)
    weight = jnp.where(digit == 0, 1.0, jnp.where(digit == 1, 256.0, jnp.where(digit == 2, -131072.0, 0.0)))
    keys = lax.dot_general(extra[:, 0:BLOCK], weight.astype(jnp.bfloat16), (((0,), (0,)), ((), ())),
                           preferred_element_type=jnp.float32)
    return keys + 131072.0


def lane_tiles(values):
    return functools.reduce(jnp.maximum, [values[:, n:n + 128] for n in range(0, BLOCK, 128)])


def halves(refs):
    if len(refs) == 1:
        return refs[0].at[0:PART], refs[0].at[FIRST:FIRST + PART]
    return refs[0].at[0:PART], refs[1]


def scores_of(left, right):
    return lax.dot_general(left, right, NT, preferred_element_type=jnp.float32)


class Whole:
    def __init__(self, wanted, held, sems):
        self.copies = []
        for i, refs in enumerate(wanted):
            for n, part in enumerate(halves(refs)):
                self.copies.append(
                    pltpu.make_async_copy(part, held.at[i, n * PART:(n + 1) * PART], sems.at[2 * i + n]))
        for copy in self.copies:
            copy.start()

    def wait(self, i):
        self.copies[2 * i].wait()
        self.copies[2 * i + 1].wait()


NAMES = ("own", "up", "um", "uo", "yp", "yo")


def by_group(row):
    empty = jnp.zeros((1, 128 - CAPACITY), jnp.float32)
    return jnp.concatenate(
        [jnp.concatenate([row[:, n * CAPACITY:(n + 1) * CAPACITY], empty], axis=1) for n in range(GROUPS)], axis=0)


def compare_kernel(sizes, products, ready, before_ref, *refs):
    sources = {}
    for block, size in sizes:
        sources[block], refs = refs[:size], refs[size:]
    out_refs, (held, sems) = refs[:-2], refs[-2:]
    whole = Whole([sources[columns] for columns, _ in products], held, sems)
    extras = {block: refs_of[0][PART:FIRST, :] for block, refs_of in sources.items()}
    found = {}

    def note(name, values):
        found[name] = jnp.maximum(found[name], values) if name in found else values

    for i, (columns, uses) in enumerate(products):
        theirs = column_keys(extras[columns])
        columns_best = jnp.full((8, BLOCK), -1.0, jnp.float32)
        whole.wait(i)
        for rows, for_rows, for_columns in uses:
            keys = row_keys(extras[rows])
            rows_best = []
            for part, r in zip(halves(sources[rows]), (0, PART)):
                own = jnp.concatenate([keys[r:r + PART, :]] * (BLOCK // 128), axis=1)
                scores = scores_of(part[...], held[i])
                earlier = theirs < own
                if for_rows:
                    rows_best.append(lane_tiles(jnp.where(earlier, scores, -1.0)))
                if for_columns:
                    later = jnp.where(earlier, -1.0, scores)
                    columns_best = jnp.maximum(columns_best, jnp.max(later.reshape(PART // 8, 8, BLOCK), axis=0))
            if for_rows:
                note(rows, jnp.max(jnp.transpose(jnp.concatenate(rows_best, axis=0)), axis=0, keepdims=True))
        if any(use[2] for use in uses):
            note(columns, jnp.max(columns_best, axis=0, keepdims=True))
    for n, name in enumerate(NAMES):
        values = before_ref[n:n + 1, :]
        if name in found:
            values = jnp.maximum(values, found[name])
        if name in ready:
            out_refs[1 + ready.index(name)][...] = by_group(values)
        out_refs[0][n:n + 1, :] = values


def compare(blocks, before, products, name, ready=()):
    names = []
    for columns, uses in products:
        for block in [columns] + [use[0] for use in uses]:
            if block not in names:
                names.append(block)
    units = sum(len(uses) for _, uses in products)
    shape = jax.ShapeDtypeStruct((GROUPS, 128), jnp.float32)
    return pl.pallas_call(
        functools.partial(compare_kernel, [(block, len(blocks[block])) for block in names], products, ready),
        out_shape=(jax.ShapeDtypeStruct((8, BLOCK), jnp.float32),) + (shape,) * len(ready),
        in_specs=[VMEM] * (1 + sum(len(blocks[block]) for block in names)),
        out_specs=(VMEM,) * (1 + len(ready)),
        scratch_shapes=[
            pltpu.VMEM((len(products), BLOCK, FEATURES), jnp.bfloat16),
            pltpu.SemaphoreType.DMA((2 * len(products),)),
        ],
        compiler_params=pltpu.CompilerParams(vmem_limit_bytes=36 * MIB),
        cost_estimate=pl.CostEstimate(flops=2 * units * BLOCK * BLOCK * FEATURES,
                                      bytes_accessed=2 * BLOCK * FEATURES, transcendentals=0),
        name=name,
    )(before, *[part for block in names for part in blocks[block]])


def finish_kernel(place_ref, kept_ref, got_ref, out_ref):
    rows = [kept_ref[CORES * n:CORES * n + 1, :] for n in range(SIDE)]
    rows = rows + [got_ref[CORES * n + 1:CORES * n + 2, :] for n in range(SIDE)]
    columns = jnp.transpose(jnp.concatenate(rows + [jnp.zeros((128 - GROUPS, 128), jnp.float32)], axis=0))
    best = jnp.full((128, ROWS), -2.0, jnp.float32)
    here = lax.broadcasted_iota(jnp.int32, (128, ROWS), 0)
    for n in range(GROUPS):
        best = jnp.where(here == place_ref[...] - 128 * n, columns[:, n:n + 1], best)
    out_ref[...] = jnp.max(best, axis=0, keepdims=True)


def device_at(x, y, z, core):
    return (z * CORES + core) * SIDE * SIDE + y * SIDE + x


def everywhere():
    return [(x, y, z, core) for z in range(SIDE) for core in range(CORES) for y in range(SIDE) for x in range(SIDE)]


def move(value, along, up):
    pairs = []
    for x, y, z, core in everywhere():
        dx, dy, dz = (0, -up, along) if core else (along, up, 0)
        pairs.append((device_at(x, y, z, core), device_at((x + dx) % SIDE, (y + dy) % SIDE, (z + dz) % SIDE, core)))
    return lax.ppermute(value, AXES, pairs)


def swap(value):
    pairs = [(device_at(x, y, z, core), device_at(x, y, z, 1 - core)) for x, y, z, core in everywhere()]
    return lax.ppermute(value, AXES, pairs)


def climb(value, planes):
    pairs = []
    for x, y, z, core in everywhere():
        dx, dz = (planes, 0) if core else (0, planes)
        pairs.append((device_at(x, y, z, core), device_at((x + dx) % SIDE, y, (z + dz) % SIDE, core)))
    return lax.ppermute(value, AXES, pairs)


def exchange(value):
    span = range(SIDE)
    lines = [[device_at(x, y, z, 0) for z in span] for x in span for y in span]
    lines = lines + [[device_at(x, y, z, 1) for x in span] for z in span for y in span]
    return lax.all_to_all(value, AXES, split_axis=0, concat_axis=0, tiled=True, axis_index_groups=lines)


def per_device(embeddings, labels, row_ids):
    keep, give, place = prepare(embeddings, labels.reshape(1, ROWS), row_ids.reshape(1, ROWS))
    pieces = join(keep, swap(give))
    own = gather([climb(piece, n) if n else piece for n, piece in enumerate(pieces)])
    yp, up, um = move(own, 0, -1), move(own, -1, 0), move(own, 1, 0)
    best = jnp.full((8, BLOCK), -1.0, jnp.float32)
    best, = compare(dict(own=(own,)), best, (("own", (("own", True, False),)),), "compare_own")
    yp, best = lax.optimization_barrier((yp, best))
    yo = move(yp, 0, -1)
    uo = move(up[0:FIRST], -1, 0), move(um[FIRST:FIRST + PART], 1, 0)
    blocks = dict(own=(own,), up=(up,), um=(um,), uo=uo, yp=(yp,), yo=(yo,))
    best, for_um = compare(blocks, best, (
        ("own", (("up", True, True),)),
        ("yp", (("own", True, True), ("up", True, True), ("um", True, True))),
    ), "compare_near", ("um",))
    for_um, best = lax.optimization_barrier((move(for_um, -1, 0), best))
    best, for_uo, for_yp = compare(blocks, best, (
        ("own", (("uo", False, True),)),
        ("yp", (("uo", True, True),)),
    ), "compare_line", ("uo", "yp"))
    back = [for_um, move(for_uo, 2, 0), move(for_yp, 0, 1)]
    best, found, for_up, for_yo = compare(blocks, best, (
        ("yo", (("own", True, False), ("up", True, True), ("uo", False, True))),
    ), "compare_far", ("own", "up", "yo"))
    for_up, for_yo, *back = lax.optimization_barrier((for_up, for_yo, *back))
    back = back + [move(for_up, 1, 0), move(for_yo, 0, 2)]
    found = functools.reduce(jnp.maximum, back, found)
    kept = exchange(found)
    out = pl.pallas_call(
        finish_kernel, out_shape=jax.ShapeDtypeStruct((1, ROWS), jnp.float32), name="finish",
    )(place, kept, swap(kept))
    return out.reshape(ROWS)


def solution(mesh):
    placed = (P(AXES, None), P(AXES, None), P(AXES))
    return jax.shard_map(
        per_device, mesh=mesh, in_specs=placed, out_specs=P(AXES), check_vma=False
    )
```

```python
import functools
import jax
import jax.numpy as jnp
from jax import lax
from jax.experimental import pallas as pl
from jax.experimental.pallas import tpu as pltpu
from jax.sharding import PartitionSpec as P

SIDE = 4
CORES = 2
ROWS = 512
FEATURES = 1024
GROUPS = 8
CAPACITY = 96
EXTRA = 16
SENT = CAPACITY + EXTRA
JOINED = CORES * CAPACITY + EXTRA
BLOCK = GROUPS * CAPACITY
PART = BLOCK // 2
FIRST = PART + EXTRA
MIB = 1 << 20
AXES = ("group", "block")
VMEM = pl.BlockSpec(memory_space=pltpu.VMEM)
NT = (((1,), (1,)), ((), ()))


def column_of(row):
    return jnp.transpose(jnp.broadcast_to(row, (128, row.shape[1])))


def spread(row, lanes):
    return jnp.concatenate([column_of(row)] * (lanes // 128), axis=1)


def prepare_kernel(emb_ref, key_ref, keep_ref, give_ref, place_ref, normed_ref):
    labels = key_ref[...] >> 16
    ids = key_ref[...] & 65535
    group = lax.axis_index("group")
    core, x, z = group & 1, lax.axis_index("block") & (SIDE - 1), group >> 1
    before = lax.broadcasted_iota(jnp.int32, (ROWS, ROWS), 0) < lax.broadcasted_iota(jnp.int32, (ROWS, ROWS), 1)
    alike = spread(labels, ROWS) == labels
    rank = jnp.sum((before & alike).astype(jnp.int32), axis=0, keepdims=True)
    plane = labels & (SIDE - 1)
    other = (labels >> 2) != core
    target = plane * SENT + rank

    def pick(target, count):
        return (lax.broadcasted_iota(jnp.int32, (count, ROWS), 0) == target).astype(jnp.bfloat16)

    slot = plane + jnp.where(other, SIDE, 0)
    place_ref[...] = slot * 128 + rank
    kind = lax.broadcasted_iota(jnp.int32, (8, ROWS), 0)
    digits = jnp.where(kind == 0, ids & 255, jnp.where(kind == 1, ids >> 8, jnp.where(kind == 2, 1, 0)))
    digits = jnp.concatenate([jnp.where(slot == n, digits, 0) for n in range(GROUPS)], axis=0)
    lane = jnp.where(labels < SIDE, z, x) * (CORES * CAPACITY) + jnp.where(other, CAPACITY, 0) + rank
    digits = lax.dot_general(digits.astype(jnp.float32).astype(jnp.bfloat16), pick(lane, FEATURES), NT,
                             preferred_element_type=jnp.float32)
    values = emb_ref[...]
    scale = lax.rsqrt(jnp.sum(values * values, axis=1, keepdims=True) + 1e-06)
    normed_ref[...] = (values * scale).astype(jnp.bfloat16)
    for out_ref, chosen, first in ((give_ref, other, SIDE), (keep_ref, jnp.logical_not(other), 0)):
        moved = jnp.dot(pick(jnp.where(chosen, target, -1), SIDE * SENT), normed_ref[...],
                        preferred_element_type=jnp.float32)
        out_ref[...] = moved.astype(jnp.bfloat16)
        for n in range(SIDE):
            extra = jnp.concatenate(
                [digits[8 * (first + n):8 * (first + n) + 8], jnp.zeros((8, FEATURES), jnp.float32)], axis=0)
            out_ref[n * SENT + CAPACITY:(n + 1) * SENT, :] = extra.astype(jnp.bfloat16)


def prepare(embeddings, keys):
    return pl.pallas_call(
        prepare_kernel,
        out_shape=(
            jax.ShapeDtypeStruct((SIDE * SENT, FEATURES), jnp.bfloat16),
            jax.ShapeDtypeStruct((SIDE * SENT, FEATURES), jnp.bfloat16),
            jax.ShapeDtypeStruct((1, ROWS), jnp.int32),
        ),
        in_specs=[VMEM] * 2,
        out_specs=(VMEM,) * 3,
        scratch_shapes=[pltpu.VMEM((ROWS, FEATURES), jnp.bfloat16)],
        compiler_params=pltpu.CompilerParams(vmem_limit_bytes=32 * MIB),
        name="prepare",
    )(embeddings, keys)


def plane():
    group = lax.axis_index("group")
    return jnp.where((group & 1) == 1, lax.axis_index("block") & (SIDE - 1), group >> 1)


def join_kernel(keep_ref, got_ref, *out_refs):
    for n in range(SIDE):
        start = ((plane() + n) & (SIDE - 1)) * SENT
        extra = jnp.zeros((EXTRA, FEATURES), jnp.float32)
        for i, ref in enumerate((keep_ref, got_ref)):
            rows = ref[pl.ds(pl.multiple_of(start, 16), CAPACITY), :]
            out_refs[n][i * CAPACITY:(i + 1) * CAPACITY, :] = rows
            extra = extra + ref[pl.ds(pl.multiple_of(start + CAPACITY, 16), EXTRA), :].astype(jnp.float32)
        out_refs[n][JOINED - EXTRA:JOINED, :] = extra.astype(jnp.bfloat16)


def join(keep, got):
    return pl.pallas_call(
        join_kernel,
        out_shape=(jax.ShapeDtypeStruct((JOINED, FEATURES), jnp.bfloat16),) * SIDE,
        in_specs=[VMEM] * 2, out_specs=(VMEM,) * SIDE,
        compiler_params=pltpu.CompilerParams(vmem_limit_bytes=16 * MIB),
        name="join",
    )(keep, got)


def gather_kernel(*refs):
    out_ref = refs[SIDE]
    extra = jnp.zeros((EXTRA, FEATURES), jnp.float32)
    size = CORES * CAPACITY
    for n in range(SIDE):
        source = (plane() - n) & (SIDE - 1)
        start = source * size + (source >> 1) * EXTRA
        out_ref[pl.ds(pl.multiple_of(start, 16), size), :] = refs[n][0:size, :]
        extra = extra + refs[n][size:JOINED, :].astype(jnp.float32)
    out_ref[PART:FIRST, :] = extra.astype(jnp.bfloat16)


def gather(pieces):
    return pl.pallas_call(
        gather_kernel,
        out_shape=jax.ShapeDtypeStruct((BLOCK + EXTRA, FEATURES), jnp.bfloat16),
        in_specs=[VMEM] * SIDE, out_specs=VMEM,
        compiler_params=pltpu.CompilerParams(vmem_limit_bytes=16 * MIB),
        name="gather",
    )(*pieces)


def column_keys(extra):
    digits = extra[:, 0:BLOCK].astype(jnp.float32)
    return digits[0:1] + digits[1:2] * 256.0 + (1.0 - digits[2:3]) * 131072.0


def row_keys(extra):
    digit = lax.broadcasted_iota(jnp.int32, (EXTRA, 128), 0)
    weight = jnp.where(digit == 0, 1.0, jnp.where(digit == 1, 256.0, jnp.where(digit == 2, -131072.0, 0.0)))
    keys = lax.dot_general(extra[:, 0:BLOCK], weight.astype(jnp.bfloat16), (((0,), (0,)), ((), ())),
                           preferred_element_type=jnp.float32)
    return keys + 131072.0


def lane_tiles(values):
    return functools.reduce(jnp.maximum, [values[:, n:n + 128] for n in range(0, BLOCK, 128)])


def halves(refs):
    if len(refs) == 1:
        return refs[0].at[0:PART], refs[0].at[FIRST:FIRST + PART]
    return refs[0].at[0:PART], refs[1]


def scores_of(left, right):
    return lax.dot_general(left, right, NT, preferred_element_type=jnp.float32)


class Whole:
    def __init__(self, wanted, held, sems):
        self.copies = []
        for i, refs in enumerate(wanted):
            for n, part in enumerate(halves(refs)):
                self.copies.append(
                    pltpu.make_async_copy(part, held.at[i, n * PART:(n + 1) * PART], sems.at[2 * i + n]))
        for copy in self.copies:
            copy.start()

    def wait(self, i):
        self.copies[2 * i].wait()
        self.copies[2 * i + 1].wait()


NAMES = ("own", "up", "um", "uo", "yp", "yo")


def by_group(row):
    empty = jnp.zeros((1, 128 - CAPACITY), jnp.float32)
    return jnp.concatenate(
        [jnp.concatenate([row[:, n * CAPACITY:(n + 1) * CAPACITY], empty], axis=1) for n in range(GROUPS)], axis=0)


def compare_kernel(sizes, products, ready, before_ref, *refs):
    sources = {}
    for block, size in sizes:
        sources[block], refs = refs[:size], refs[size:]
    out_refs, (held, sems) = refs[:-2], refs[-2:]
    whole = Whole([sources[columns] for columns, _ in products], held, sems)
    extras = {block: refs_of[0][PART:FIRST, :] for block, refs_of in sources.items()}
    found = {}

    def note(name, values):
        found[name] = jnp.maximum(found[name], values) if name in found else values

    for i, (columns, uses) in enumerate(products):
        theirs = column_keys(extras[columns])
        columns_best = jnp.full((8, BLOCK), -1.0, jnp.float32)
        whole.wait(i)
        for rows, for_rows, for_columns in uses:
            keys = row_keys(extras[rows])
            rows_best = []
            for part, r in zip(halves(sources[rows]), (0, PART)):
                own = jnp.concatenate([keys[r:r + PART, :]] * (BLOCK // 128), axis=1)
                scores = scores_of(part[...], held[i])
                earlier = theirs < own
                if for_rows:
                    rows_best.append(lane_tiles(jnp.where(earlier, scores, -1.0)))
                if for_columns:
                    later = jnp.where(earlier, -1.0, scores)
                    columns_best = jnp.maximum(columns_best, jnp.max(later.reshape(PART // 8, 8, BLOCK), axis=0))
            if for_rows:
                note(rows, jnp.max(jnp.transpose(jnp.concatenate(rows_best, axis=0)), axis=0, keepdims=True))
        if any(use[2] for use in uses):
            note(columns, jnp.max(columns_best, axis=0, keepdims=True))
    for n, name in enumerate(NAMES):
        values = before_ref[n:n + 1, :]
        if name in found:
            values = jnp.maximum(values, found[name])
        if name in ready:
            out_refs[1 + ready.index(name)][...] = by_group(values)
        out_refs[0][n:n + 1, :] = values


def compare(blocks, before, products, name, ready=()):
    names = []
    for columns, uses in products:
        for block in [columns] + [use[0] for use in uses]:
            if block not in names:
                names.append(block)
    units = sum(len(uses) for _, uses in products)
    shape = jax.ShapeDtypeStruct((GROUPS, 128), jnp.float32)
    return pl.pallas_call(
        functools.partial(compare_kernel, [(block, len(blocks[block])) for block in names], products, ready),
        out_shape=(jax.ShapeDtypeStruct((8, BLOCK), jnp.float32),) + (shape,) * len(ready),
        in_specs=[VMEM] * (1 + sum(len(blocks[block]) for block in names)),
        out_specs=(VMEM,) * (1 + len(ready)),
        scratch_shapes=[
            pltpu.VMEM((len(products), BLOCK, FEATURES), jnp.bfloat16),
            pltpu.SemaphoreType.DMA((2 * len(products),)),
        ],
        compiler_params=pltpu.CompilerParams(vmem_limit_bytes=36 * MIB),
        cost_estimate=pl.CostEstimate(flops=2 * units * BLOCK * BLOCK * FEATURES,
                                      bytes_accessed=2 * BLOCK * FEATURES, transcendentals=0),
        name=name,
    )(before, *[part for block in names for part in blocks[block]])


def finish_kernel(place_ref, kept_ref, got_ref, out_ref):
    rows = [kept_ref[CORES * n:CORES * n + 1, :] for n in range(SIDE)]
    rows = rows + [got_ref[CORES * n + 1:CORES * n + 2, :] for n in range(SIDE)]
    columns = jnp.transpose(jnp.concatenate(rows + [jnp.zeros((128 - GROUPS, 128), jnp.float32)], axis=0))
    best = jnp.full((128, ROWS), -2.0, jnp.float32)
    here = lax.broadcasted_iota(jnp.int32, (128, ROWS), 0)
    for n in range(GROUPS):
        best = jnp.where(here == place_ref[...] - 128 * n, columns[:, n:n + 1], best)
    out_ref[...] = jnp.max(best, axis=0, keepdims=True)


def device_at(x, y, z, core):
    return (z * CORES + core) * SIDE * SIDE + y * SIDE + x


def everywhere():
    return [(x, y, z, core) for z in range(SIDE) for core in range(CORES) for y in range(SIDE) for x in range(SIDE)]


def move(value, along, up):
    pairs = []
    for x, y, z, core in everywhere():
        dx, dy, dz = (0, -up, along) if core else (along, up, 0)
        pairs.append((device_at(x, y, z, core), device_at((x + dx) % SIDE, (y + dy) % SIDE, (z + dz) % SIDE, core)))
    return lax.ppermute(value, AXES, pairs)


def swap(value):
    pairs = [(device_at(x, y, z, core), device_at(x, y, z, 1 - core)) for x, y, z, core in everywhere()]
    return lax.ppermute(value, AXES, pairs)


def climb(value, planes):
    pairs = []
    for x, y, z, core in everywhere():
        dx, dz = (planes, 0) if core else (0, planes)
        pairs.append((device_at(x, y, z, core), device_at((x + dx) % SIDE, y, (z + dz) % SIDE, core)))
    return lax.ppermute(value, AXES, pairs)


def exchange(value):
    span = range(SIDE)
    lines = [[device_at(x, y, z, 0) for z in span] for x in span for y in span]
    lines = lines + [[device_at(x, y, z, 1) for x in span] for z in span for y in span]
    return lax.all_to_all(value, AXES, split_axis=0, concat_axis=0, tiled=True, axis_index_groups=lines)


def per_device(embeddings, labels, row_ids):
    keys = labels.reshape(ROWS) * 65536 + row_ids
    keep, give, place = prepare(embeddings, keys.reshape(1, ROWS))
    pieces = join(keep, swap(give))
    own = gather([climb(piece, n) if n else piece for n, piece in enumerate(pieces)])
    yp, up, um = move(own, 0, -1), move(own, -1, 0), move(own, 1, 0)
    best = jnp.full((8, BLOCK), -1.0, jnp.float32)
    best, = compare(dict(own=(own,)), best, (("own", (("own", True, False),)),), "compare_own")
    yp, best = lax.optimization_barrier((yp, best))
    yo = move(yp, 0, -1)
    uo = move(up[0:FIRST], -1, 0), move(um[FIRST:FIRST + PART], 1, 0)
    blocks = dict(own=(own,), up=(up,), um=(um,), uo=uo, yp=(yp,), yo=(yo,))
    best, for_um = compare(blocks, best, (
        ("own", (("up", True, True),)),
        ("yp", (("own", True, True), ("up", True, True), ("um", True, True))),
    ), "compare_near", ("um",))
    for_um, best = lax.optimization_barrier((move(for_um, -1, 0), best))
    best, for_uo, for_yp = compare(blocks, best, (
        ("own", (("uo", False, True),)),
        ("yp", (("uo", True, True),)),
    ), "compare_line", ("uo", "yp"))
    back = [for_um, move(for_uo, 2, 0), move(for_yp, 0, 1)]
    best, found, for_up, for_yo = compare(blocks, best, (
        ("yo", (("own", True, False), ("up", True, True), ("uo", False, True))),
    ), "compare_far", ("own", "up", "yo"))
    for_up, for_yo, *back = lax.optimization_barrier((for_up, for_yo, *back))
    back = back + [move(for_up, 1, 0), move(for_yo, 0, 2)]
    found = functools.reduce(jnp.maximum, back, found)
    kept = exchange(found)
    out = pl.pallas_call(
        finish_kernel, out_shape=jax.ShapeDtypeStruct((1, ROWS), jnp.float32), name="finish",
        in_specs=[VMEM] * 3, out_specs=VMEM,
        compiler_params=pltpu.CompilerParams(vmem_limit_bytes=8 * MIB),
    )(place, kept, swap(kept))
    return out.reshape(ROWS)


def solution(mesh):
    placed = (P(AXES, None), P(AXES, None), P(AXES))
    return jax.shard_map(
        per_device, mesh=mesh, in_specs=placed, out_specs=P(AXES), check_vma=False
    )
```

```python
import functools
import jax
import jax.numpy as jnp
from jax import lax
from jax.experimental import pallas as pl
from jax.experimental.pallas import tpu as pltpu
from jax.sharding import PartitionSpec as P

SIDE = 4
CORES = 2
ROWS = 512
FEATURES = 1024
GROUPS = 8
CAPACITY = 96
EXTRA = 16
SENT = CAPACITY + EXTRA
BLOCK = GROUPS * CAPACITY
PART = BLOCK // 2
FIRST = PART + EXTRA
MIB = 1 << 20
AXES = ("group", "block")
VMEM = pl.BlockSpec(memory_space=pltpu.VMEM)
NT = (((1,), (1,)), ((), ()))


def column_of(row):
    return jnp.transpose(jnp.broadcast_to(row, (128, row.shape[1])))


def spread(row, lanes):
    return jnp.concatenate([column_of(row)] * (lanes // 128), axis=1)


def prepare_kernel(emb_ref, key_ref, *refs):
    keep_refs, (give_ref, place_ref, normed_ref) = refs[:SIDE], refs[SIDE:]
    labels = key_ref[...] >> 16
    ids = key_ref[...] & 65535
    group = lax.axis_index("group")
    core, x, z = group & 1, lax.axis_index("block") & (SIDE - 1), group >> 1
    before = lax.broadcasted_iota(jnp.int32, (ROWS, ROWS), 0) < lax.broadcasted_iota(jnp.int32, (ROWS, ROWS), 1)
    alike = spread(labels, ROWS) == labels
    rank = jnp.sum((before & alike).astype(jnp.int32), axis=0, keepdims=True)
    plane = labels & (SIDE - 1)
    other = (labels >> 2) != core
    turn = (plane - jnp.where(labels < SIDE, z, x)) & (SIDE - 1)
    target = turn * SENT + rank

    def pick(target, count):
        return (lax.broadcasted_iota(jnp.int32, (count, ROWS), 0) == target).astype(jnp.bfloat16)

    slot = plane + jnp.where(other, SIDE, 0)
    place_ref[...] = slot * 128 + rank
    piece = turn + jnp.where(other, SIDE, 0)
    kind = lax.broadcasted_iota(jnp.int32, (8, ROWS), 0)
    digits = jnp.where(kind == 0, ids & 255, jnp.where(kind == 1, ids >> 8, jnp.where(kind == 2, 1, 0)))
    digits = jnp.concatenate([jnp.where(piece == n, digits, 0) for n in range(GROUPS)], axis=0)
    lane = jnp.where(labels < SIDE, z, x) * (CORES * CAPACITY) + jnp.where(other, CAPACITY, 0) + rank
    digits = lax.dot_general(digits.astype(jnp.float32).astype(jnp.bfloat16), pick(lane, FEATURES), NT,
                             preferred_element_type=jnp.float32)
    values = emb_ref[...]
    scale = lax.rsqrt(jnp.sum(values * values, axis=1, keepdims=True) + 1e-06)
    normed_ref[...] = (values * scale).astype(jnp.bfloat16)
    for chosen, first in ((jnp.logical_not(other), 0), (other, SIDE)):
        moved = jnp.dot(pick(jnp.where(chosen, target, -1), SIDE * SENT), normed_ref[...],
                        preferred_element_type=jnp.float32).astype(jnp.bfloat16)
        for n in range(SIDE):
            out_ref, start = (give_ref, n * SENT) if first else (keep_refs[n], 0)
            extra = jnp.concatenate(
                [digits[8 * (first + n):8 * (first + n) + 8], jnp.zeros((8, FEATURES), jnp.float32)], axis=0)
            out_ref[start:start + CAPACITY, :] = moved[n * SENT:n * SENT + CAPACITY, :]
            out_ref[start + CAPACITY:start + SENT, :] = extra.astype(jnp.bfloat16)


def prepare(embeddings, keys):
    return pl.pallas_call(
        prepare_kernel,
        out_shape=(
            *[jax.ShapeDtypeStruct((SENT, FEATURES), jnp.bfloat16)] * SIDE,
            jax.ShapeDtypeStruct((SIDE * SENT, FEATURES), jnp.bfloat16),
            jax.ShapeDtypeStruct((1, ROWS), jnp.int32),
        ),
        in_specs=[VMEM] * 2,
        out_specs=(VMEM,) * (SIDE + 2),
        scratch_shapes=[pltpu.VMEM((ROWS, FEATURES), jnp.bfloat16)],
        compiler_params=pltpu.CompilerParams(vmem_limit_bytes=32 * MIB),
        name="prepare",
    )(embeddings, keys)


def plane():
    group = lax.axis_index("group")
    return jnp.where((group & 1) == 1, lax.axis_index("block") & (SIDE - 1), group >> 1)


def gather_kernel(*refs):
    out_ref = refs[GROUPS]
    extra = jnp.zeros((EXTRA, FEATURES), jnp.float32)
    for n in range(GROUPS):
        source = (plane() - n) & (SIDE - 1)
        start = (source * CORES + n // SIDE) * CAPACITY + (source >> 1) * EXTRA
        out_ref[pl.ds(pl.multiple_of(start, 16), CAPACITY), :] = refs[n][0:CAPACITY, :]
        extra = extra + refs[n][CAPACITY:SENT, :].astype(jnp.float32)
    out_ref[PART:FIRST, :] = extra.astype(jnp.bfloat16)


def gather(pieces):
    return pl.pallas_call(
        gather_kernel,
        out_shape=jax.ShapeDtypeStruct((BLOCK + EXTRA, FEATURES), jnp.bfloat16),
        in_specs=[VMEM] * GROUPS, out_specs=VMEM,
        compiler_params=pltpu.CompilerParams(vmem_limit_bytes=16 * MIB),
        name="gather",
    )(*pieces)


def column_keys(extra):
    digits = extra[:, 0:BLOCK].astype(jnp.float32)
    return digits[0:1] + digits[1:2] * 256.0 + (1.0 - digits[2:3]) * 131072.0


def row_keys(extra):
    digit = lax.broadcasted_iota(jnp.int32, (EXTRA, 128), 0)
    weight = jnp.where(digit == 0, 1.0, jnp.where(digit == 1, 256.0, jnp.where(digit == 2, -131072.0, 0.0)))
    keys = lax.dot_general(extra[:, 0:BLOCK], weight.astype(jnp.bfloat16), (((0,), (0,)), ((), ())),
                           preferred_element_type=jnp.float32)
    return keys + 131072.0


def lane_tiles(values):
    return functools.reduce(jnp.maximum, [values[:, n:n + 128] for n in range(0, BLOCK, 128)])


def halves(refs):
    if len(refs) == 1:
        return refs[0].at[0:PART], refs[0].at[FIRST:FIRST + PART]
    return refs[0].at[0:PART], refs[1]


def scores_of(left, right):
    return lax.dot_general(left, right, NT, preferred_element_type=jnp.float32)


class Whole:
    def __init__(self, wanted, held, sems):
        self.copies = []
        for i, refs in enumerate(wanted):
            for n, part in enumerate(halves(refs)):
                self.copies.append(
                    pltpu.make_async_copy(part, held.at[i, n * PART:(n + 1) * PART], sems.at[2 * i + n]))
        for copy in self.copies:
            copy.start()

    def wait(self, i):
        self.copies[2 * i].wait()
        self.copies[2 * i + 1].wait()


NAMES = ("own", "up", "um", "uo", "yp", "yo")


def by_group(row):
    empty = jnp.zeros((1, 128 - CAPACITY), jnp.float32)
    return jnp.concatenate(
        [jnp.concatenate([row[:, n * CAPACITY:(n + 1) * CAPACITY], empty], axis=1) for n in range(GROUPS)], axis=0)


def compare_kernel(sizes, products, ready, before_ref, *refs):
    sources = {}
    for block, size in sizes:
        sources[block], refs = refs[:size], refs[size:]
    out_refs, (held, sems) = refs[:-2], refs[-2:]
    whole = Whole([sources[columns] for columns, _ in products], held, sems)
    extras = {block: refs_of[0][PART:FIRST, :] for block, refs_of in sources.items()}
    found = {}

    def note(name, values):
        found[name] = jnp.maximum(found[name], values) if name in found else values

    for i, (columns, uses) in enumerate(products):
        theirs = column_keys(extras[columns])
        columns_best = jnp.full((8, BLOCK), -1.0, jnp.float32)
        whole.wait(i)
        for rows, for_rows, for_columns in uses:
            keys = row_keys(extras[rows])
            rows_best = []
            for part, r in zip(halves(sources[rows]), (0, PART)):
                own = jnp.concatenate([keys[r:r + PART, :]] * (BLOCK // 128), axis=1)
                scores = scores_of(part[...], held[i])
                earlier = theirs < own
                if for_rows:
                    rows_best.append(lane_tiles(jnp.where(earlier, scores, -1.0)))
                if for_columns:
                    later = jnp.where(earlier, -1.0, scores)
                    columns_best = jnp.maximum(columns_best, jnp.max(later.reshape(PART // 8, 8, BLOCK), axis=0))
            if for_rows:
                note(rows, jnp.max(jnp.transpose(jnp.concatenate(rows_best, axis=0)), axis=0, keepdims=True))
        if any(use[2] for use in uses):
            note(columns, jnp.max(columns_best, axis=0, keepdims=True))
    for n, name in enumerate(NAMES):
        values = before_ref[n:n + 1, :]
        if name in found:
            values = jnp.maximum(values, found[name])
        if name in ready:
            out_refs[1 + ready.index(name)][...] = by_group(values)
        out_refs[0][n:n + 1, :] = values


def compare(blocks, before, products, name, ready=()):
    names = []
    for columns, uses in products:
        for block in [columns] + [use[0] for use in uses]:
            if block not in names:
                names.append(block)
    units = sum(len(uses) for _, uses in products)
    shape = jax.ShapeDtypeStruct((GROUPS, 128), jnp.float32)
    return pl.pallas_call(
        functools.partial(compare_kernel, [(block, len(blocks[block])) for block in names], products, ready),
        out_shape=(jax.ShapeDtypeStruct((8, BLOCK), jnp.float32),) + (shape,) * len(ready),
        in_specs=[VMEM] * (1 + sum(len(blocks[block]) for block in names)),
        out_specs=(VMEM,) * (1 + len(ready)),
        scratch_shapes=[
            pltpu.VMEM((len(products), BLOCK, FEATURES), jnp.bfloat16),
            pltpu.SemaphoreType.DMA((2 * len(products),)),
        ],
        compiler_params=pltpu.CompilerParams(vmem_limit_bytes=36 * MIB),
        cost_estimate=pl.CostEstimate(flops=2 * units * BLOCK * BLOCK * FEATURES,
                                      bytes_accessed=2 * BLOCK * FEATURES, transcendentals=0),
        name=name,
    )(before, *[part for block in names for part in blocks[block]])


def finish_kernel(place_ref, kept_ref, got_ref, out_ref):
    rows = [kept_ref[CORES * n:CORES * n + 1, :] for n in range(SIDE)]
    rows = rows + [got_ref[CORES * n + 1:CORES * n + 2, :] for n in range(SIDE)]
    columns = jnp.transpose(jnp.concatenate(rows + [jnp.zeros((128 - GROUPS, 128), jnp.float32)], axis=0))
    best = jnp.full((128, ROWS), -2.0, jnp.float32)
    here = lax.broadcasted_iota(jnp.int32, (128, ROWS), 0)
    for n in range(GROUPS):
        best = jnp.where(here == place_ref[...] - 128 * n, columns[:, n:n + 1], best)
    out_ref[...] = jnp.max(best, axis=0, keepdims=True)


def device_at(x, y, z, core):
    return (z * CORES + core) * SIDE * SIDE + y * SIDE + x


def everywhere():
    return [(x, y, z, core) for z in range(SIDE) for core in range(CORES) for y in range(SIDE) for x in range(SIDE)]


def move(value, along, up):
    pairs = []
    for x, y, z, core in everywhere():
        dx, dy, dz = (0, -up, along) if core else (along, up, 0)
        pairs.append((device_at(x, y, z, core), device_at((x + dx) % SIDE, (y + dy) % SIDE, (z + dz) % SIDE, core)))
    return lax.ppermute(value, AXES, pairs)


def swap(value):
    pairs = [(device_at(x, y, z, core), device_at(x, y, z, 1 - core)) for x, y, z, core in everywhere()]
    return lax.ppermute(value, AXES, pairs)


def climb(value, planes):
    pairs = []
    for x, y, z, core in everywhere():
        dx, dz = (planes, 0) if core else (0, planes)
        pairs.append((device_at(x, y, z, core), device_at((x + dx) % SIDE, y, (z + dz) % SIDE, core)))
    return lax.ppermute(value, AXES, pairs)


def exchange(value):
    span = range(SIDE)
    lines = [[device_at(x, y, z, 0) for z in span] for x in span for y in span]
    lines = lines + [[device_at(x, y, z, 1) for x in span] for z in span for y in span]
    return lax.all_to_all(value, AXES, split_axis=0, concat_axis=0, tiled=True, axis_index_groups=lines)


def per_device(embeddings, labels, row_ids):
    keys = labels.reshape(ROWS) * 65536 + row_ids
    *keep, give, place = prepare(embeddings, keys.reshape(1, ROWS))
    got = swap(give)
    kept = [climb(part, n) if n else part for n, part in enumerate(keep)]
    got = [got[n * SENT:(n + 1) * SENT] for n in range(SIDE)]
    got = [climb(part, n) if n else part for n, part in enumerate(got)]
    own = gather(kept + got)
    yp, up, um = move(own, 0, -1), move(own, -1, 0), move(own, 1, 0)
    best = jnp.full((8, BLOCK), -1.0, jnp.float32)
    best, = compare(dict(own=(own,)), best, (("own", (("own", True, False),)),), "compare_own")
    yp, best = lax.optimization_barrier((yp, best))
    yo = move(yp, 0, -1)
    uo = move(up[0:FIRST], -1, 0), move(um[FIRST:FIRST + PART], 1, 0)
    blocks = dict(own=(own,), up=(up,), um=(um,), uo=uo, yp=(yp,), yo=(yo,))
    best, for_um = compare(blocks, best, (
        ("own", (("up", True, True),)),
        ("yp", (("own", True, True), ("up", True, True), ("um", True, True))),
    ), "compare_near", ("um",))
    for_um, best = lax.optimization_barrier((move(for_um, -1, 0), best))
    best, for_uo, for_yp = compare(blocks, best, (
        ("own", (("uo", False, True),)),
        ("yp", (("uo", True, True),)),
    ), "compare_line", ("uo", "yp"))
    back = [for_um, move(for_uo, 2, 0), move(for_yp, 0, 1)]
    best, found, for_up, for_yo = compare(blocks, best, (
        ("yo", (("own", True, False), ("up", True, True), ("uo", False, True))),
    ), "compare_far", ("own", "up", "yo"))
    for_up, for_yo, *back = lax.optimization_barrier((for_up, for_yo, *back))
    back = back + [move(for_up, 1, 0), move(for_yo, 0, 2)]
    found = functools.reduce(jnp.maximum, back, found)
    kept = exchange(found)
    out = pl.pallas_call(
        finish_kernel, out_shape=jax.ShapeDtypeStruct((1, ROWS), jnp.float32), name="finish",
        in_specs=[VMEM] * 3, out_specs=VMEM,
        compiler_params=pltpu.CompilerParams(vmem_limit_bytes=8 * MIB),
    )(place, kept, swap(kept))
    return out.reshape(ROWS)


def solution(mesh):
    placed = (P(AXES, None), P(AXES, None), P(AXES))
    return jax.shard_map(
        per_device, mesh=mesh, in_specs=placed, out_specs=P(AXES), check_vma=False
    )
```

```python
import functools
import jax
import jax.numpy as jnp
from jax import lax
from jax.experimental import pallas as pl
from jax.experimental.pallas import tpu as pltpu
from jax.sharding import PartitionSpec as P

SIDE = 4
CORES = 2
ROWS = 512
FEATURES = 1024
GROUPS = 8
CAPACITY = 96
EXTRA = 16
SENT = CAPACITY + EXTRA
BLOCK = GROUPS * CAPACITY
PART = BLOCK // 2
FIRST = PART + EXTRA
MIB = 1 << 20
AXES = ("group", "block")
VMEM = pl.BlockSpec(memory_space=pltpu.VMEM)
NT = (((1,), (1,)), ((), ()))


def column_of(row):
    return jnp.transpose(jnp.broadcast_to(row, (128, row.shape[1])))


def spread(row, lanes):
    return jnp.concatenate([column_of(row)] * (lanes // 128), axis=1)


def prepare_kernel(emb_ref, key_ref, *refs):
    keep_refs, (give_ref, place_ref, normed_ref) = refs[:SIDE], refs[SIDE:]
    labels = key_ref[...] >> 16
    ids = key_ref[...] & 65535
    group = lax.axis_index("group")
    core, x, z = group & 1, lax.axis_index("block") & (SIDE - 1), group >> 1
    before = lax.broadcasted_iota(jnp.int32, (ROWS, ROWS), 0) < lax.broadcasted_iota(jnp.int32, (ROWS, ROWS), 1)
    alike = spread(labels, ROWS) == labels
    rank = jnp.sum((before & alike).astype(jnp.int32), axis=0, keepdims=True)
    plane = labels & (SIDE - 1)
    other = (labels >> 2) != core
    turn = (plane - jnp.where(labels < SIDE, z, x)) & (SIDE - 1)
    target = turn * SENT + rank

    def pick(target, count):
        return (lax.broadcasted_iota(jnp.int32, (count, ROWS), 0) == target).astype(jnp.bfloat16)

    slot = plane + jnp.where(other, SIDE, 0)
    place_ref[...] = slot * 128 + rank
    piece = turn + jnp.where(other, SIDE, 0)
    kind = lax.broadcasted_iota(jnp.int32, (8, ROWS), 0)
    digits = jnp.where(kind == 0, ids & 255, jnp.where(kind == 1, ids >> 8, jnp.where(kind == 2, 1, 0)))
    digits = jnp.concatenate([jnp.where(piece == n, digits, 0) for n in range(GROUPS)], axis=0)
    lane = jnp.where(labels < SIDE, z, x) * (CORES * CAPACITY) + jnp.where(other, CAPACITY, 0) + rank
    digits = lax.dot_general(digits.astype(jnp.float32).astype(jnp.bfloat16), pick(lane, FEATURES), NT,
                             preferred_element_type=jnp.float32)
    values = emb_ref[...]
    scale = lax.rsqrt(jnp.sum(values * values, axis=1, keepdims=True) + 1e-06)
    normed_ref[...] = (values * scale).astype(jnp.bfloat16)
    for chosen, first in ((jnp.logical_not(other), 0), (other, SIDE)):
        moved = jnp.dot(pick(jnp.where(chosen, target, -1), SIDE * SENT), normed_ref[...],
                        preferred_element_type=jnp.float32).astype(jnp.bfloat16)
        for n in range(SIDE):
            out_ref, start = (give_ref, n * SENT) if first else (keep_refs[n], 0)
            extra = jnp.concatenate(
                [digits[8 * (first + n):8 * (first + n) + 8], jnp.zeros((8, FEATURES), jnp.float32)], axis=0)
            out_ref[start:start + CAPACITY, :] = moved[n * SENT:n * SENT + CAPACITY, :]
            out_ref[start + CAPACITY:start + SENT, :] = extra.astype(jnp.bfloat16)


def prepare(embeddings, keys):
    return pl.pallas_call(
        prepare_kernel,
        out_shape=(
            *[jax.ShapeDtypeStruct((SENT, FEATURES), jnp.bfloat16)] * SIDE,
            jax.ShapeDtypeStruct((SIDE * SENT, FEATURES), jnp.bfloat16),
            jax.ShapeDtypeStruct((1, ROWS), jnp.int32),
        ),
        in_specs=[VMEM] * 2,
        out_specs=(VMEM,) * (SIDE + 2),
        scratch_shapes=[pltpu.VMEM((ROWS, FEATURES), jnp.bfloat16)],
        compiler_params=pltpu.CompilerParams(vmem_limit_bytes=32 * MIB),
        name="prepare",
    )(embeddings, keys)


def plane():
    group = lax.axis_index("group")
    return jnp.where((group & 1) == 1, lax.axis_index("block") & (SIDE - 1), group >> 1)


def gather_kernel(*refs):
    out_ref = refs[GROUPS]
    extra = jnp.zeros((EXTRA, FEATURES), jnp.float32)
    for n in range(GROUPS):
        source = (plane() - n) & (SIDE - 1)
        start = (source * CORES + n // SIDE) * CAPACITY + (source >> 1) * EXTRA
        out_ref[pl.ds(pl.multiple_of(start, 16), CAPACITY), :] = refs[n][0:CAPACITY, :]
        extra = extra + refs[n][CAPACITY:SENT, :].astype(jnp.float32)
    out_ref[PART:FIRST, :] = extra.astype(jnp.bfloat16)


def gather(pieces):
    return pl.pallas_call(
        gather_kernel,
        out_shape=jax.ShapeDtypeStruct((BLOCK + EXTRA, FEATURES), jnp.bfloat16),
        in_specs=[VMEM] * GROUPS, out_specs=VMEM,
        compiler_params=pltpu.CompilerParams(vmem_limit_bytes=16 * MIB),
        name="gather",
    )(*pieces)


def column_keys(extra):
    digits = extra[:, 0:BLOCK].astype(jnp.float32)
    return digits[0:1] + digits[1:2] * 256.0 + (1.0 - digits[2:3]) * 131072.0


def row_keys(extra):
    digit = lax.broadcasted_iota(jnp.int32, (EXTRA, 128), 0)
    weight = jnp.where(digit == 0, 1.0, jnp.where(digit == 1, 256.0, jnp.where(digit == 2, -131072.0, 0.0)))
    keys = lax.dot_general(extra[:, 0:BLOCK], weight.astype(jnp.bfloat16), (((0,), (0,)), ((), ())),
                           preferred_element_type=jnp.float32)
    return keys + 131072.0


def lane_tiles(values):
    return functools.reduce(jnp.maximum, [values[:, n:n + 128] for n in range(0, BLOCK, 128)])


def halves(refs):
    if len(refs) == 1:
        return refs[0].at[0:PART], refs[0].at[FIRST:FIRST + PART]
    return refs[0].at[0:PART], refs[1]


def scores_of(left, right):
    return lax.dot_general(left, right, NT, preferred_element_type=jnp.float32)


class Whole:
    def __init__(self, wanted, held, sems):
        self.copies = []
        for i, refs in enumerate(wanted):
            for n, part in enumerate(halves(refs)):
                self.copies.append(
                    pltpu.make_async_copy(part, held.at[i, n * PART:(n + 1) * PART], sems.at[2 * i + n]))
        for copy in self.copies:
            copy.start()

    def wait(self, i):
        self.copies[2 * i].wait()
        self.copies[2 * i + 1].wait()


NAMES = ("own", "up", "um", "uo", "yp", "yo")


def by_group(row):
    empty = jnp.zeros((1, 128 - CAPACITY), jnp.float32)
    return jnp.concatenate(
        [jnp.concatenate([row[:, n * CAPACITY:(n + 1) * CAPACITY], empty], axis=1) for n in range(GROUPS)], axis=0)


def compare_kernel(sizes, products, ready, before_ref, *refs):
    sources = {}
    for block, size in sizes:
        sources[block], refs = refs[:size], refs[size:]
    out_refs, (held, sems) = refs[:-2], refs[-2:]
    whole = Whole([sources[columns] for columns, _ in products], held, sems)
    extras = {block: refs_of[0][PART:FIRST, :] for block, refs_of in sources.items()}
    found, row_keys_of = {}, {}

    def note(name, values):
        found[name] = jnp.maximum(found[name], values) if name in found else values

    for i, (columns, uses) in enumerate(products):
        theirs = column_keys(extras[columns])
        columns_best = jnp.full((8, BLOCK), -1.0, jnp.float32)
        whole.wait(i)
        for rows, for_rows, for_columns in uses:
            if rows not in row_keys_of:
                row_keys_of[rows] = row_keys(extras[rows])
            keys = row_keys_of[rows]
            rows_best = []
            for part, r in zip(halves(sources[rows]), (0, PART)):
                own = jnp.concatenate([keys[r:r + PART, :]] * (BLOCK // 128), axis=1)
                scores = scores_of(part[...], held[i])
                earlier = theirs < own
                if for_rows:
                    rows_best.append(lane_tiles(jnp.where(earlier, scores, -1.0)))
                if for_columns:
                    later = jnp.where(earlier, -1.0, scores)
                    columns_best = jnp.maximum(columns_best, jnp.max(later.reshape(PART // 8, 8, BLOCK), axis=0))
            if for_rows:
                note(rows, jnp.max(jnp.transpose(jnp.concatenate(rows_best, axis=0)), axis=0, keepdims=True))
        if any(use[2] for use in uses):
            note(columns, jnp.max(columns_best, axis=0, keepdims=True))
    for n, name in enumerate(NAMES):
        values = before_ref[n:n + 1, :]
        if name in found:
            values = jnp.maximum(values, found[name])
        if name in ready:
            out_refs[1 + ready.index(name)][...] = by_group(values)
        out_refs[0][n:n + 1, :] = values


def compare(blocks, before, products, name, ready=()):
    names = []
    for columns, uses in products:
        for block in [columns] + [use[0] for use in uses]:
            if block not in names:
                names.append(block)
    units = sum(len(uses) for _, uses in products)
    shape = jax.ShapeDtypeStruct((GROUPS, 128), jnp.float32)
    return pl.pallas_call(
        functools.partial(compare_kernel, [(block, len(blocks[block])) for block in names], products, ready),
        out_shape=(jax.ShapeDtypeStruct((8, BLOCK), jnp.float32),) + (shape,) * len(ready),
        in_specs=[VMEM] * (1 + sum(len(blocks[block]) for block in names)),
        out_specs=(VMEM,) * (1 + len(ready)),
        scratch_shapes=[
            pltpu.VMEM((len(products), BLOCK, FEATURES), jnp.bfloat16),
            pltpu.SemaphoreType.DMA((2 * len(products),)),
        ],
        compiler_params=pltpu.CompilerParams(vmem_limit_bytes=36 * MIB),
        cost_estimate=pl.CostEstimate(flops=2 * units * BLOCK * BLOCK * FEATURES,
                                      bytes_accessed=2 * BLOCK * FEATURES, transcendentals=0),
        name=name,
    )(before, *[part for block in names for part in blocks[block]])


def finish_kernel(place_ref, kept_ref, got_ref, out_ref):
    rows = [kept_ref[CORES * n:CORES * n + 1, :] for n in range(SIDE)]
    rows = rows + [got_ref[CORES * n + 1:CORES * n + 2, :] for n in range(SIDE)]
    columns = jnp.transpose(jnp.concatenate(rows + [jnp.zeros((128 - GROUPS, 128), jnp.float32)], axis=0))
    best = jnp.full((128, ROWS), -2.0, jnp.float32)
    here = lax.broadcasted_iota(jnp.int32, (128, ROWS), 0)
    for n in range(GROUPS):
        best = jnp.where(here == place_ref[...] - 128 * n, columns[:, n:n + 1], best)
    out_ref[...] = jnp.max(best, axis=0, keepdims=True)


def device_at(x, y, z, core):
    return (z * CORES + core) * SIDE * SIDE + y * SIDE + x


def everywhere():
    return [(x, y, z, core) for z in range(SIDE) for core in range(CORES) for y in range(SIDE) for x in range(SIDE)]


def move(value, along, up):
    pairs = []
    for x, y, z, core in everywhere():
        dx, dy, dz = (0, -up, along) if core else (along, up, 0)
        pairs.append((device_at(x, y, z, core), device_at((x + dx) % SIDE, (y + dy) % SIDE, (z + dz) % SIDE, core)))
    return lax.ppermute(value, AXES, pairs)


def swap(value):
    pairs = [(device_at(x, y, z, core), device_at(x, y, z, 1 - core)) for x, y, z, core in everywhere()]
    return lax.ppermute(value, AXES, pairs)


def climb(value, planes):
    pairs = []
    for x, y, z, core in everywhere():
        dx, dz = (planes, 0) if core else (0, planes)
        pairs.append((device_at(x, y, z, core), device_at((x + dx) % SIDE, y, (z + dz) % SIDE, core)))
    return lax.ppermute(value, AXES, pairs)


def exchange(value):
    span = range(SIDE)
    lines = [[device_at(x, y, z, 0) for z in span] for x in span for y in span]
    lines = lines + [[device_at(x, y, z, 1) for x in span] for z in span for y in span]
    return lax.all_to_all(value, AXES, split_axis=0, concat_axis=0, tiled=True, axis_index_groups=lines)


def per_device(embeddings, labels, row_ids):
    keys = labels.reshape(ROWS) * 65536 + row_ids
    *keep, give, place = prepare(embeddings, keys.reshape(1, ROWS))
    got = swap(give)
    kept = [climb(part, n) if n else part for n, part in enumerate(keep)]
    got = [got[n * SENT:(n + 1) * SENT] for n in range(SIDE)]
    got = [climb(part, n) if n else part for n, part in enumerate(got)]
    own = gather(kept + got)
    yp, up, um = move(own, 0, -1), move(own, -1, 0), move(own, 1, 0)
    best = jnp.full((8, BLOCK), -1.0, jnp.float32)
    best, = compare(dict(own=(own,)), best, (("own", (("own", True, False),)),), "compare_own")
    yp, best = lax.optimization_barrier((yp, best))
    yo = move(yp, 0, -1)
    uo = move(up[0:FIRST], -1, 0), move(um[FIRST:FIRST + PART], 1, 0)
    blocks = dict(own=(own,), up=(up,), um=(um,), uo=uo, yp=(yp,), yo=(yo,))
    best, for_um = compare(blocks, best, (
        ("own", (("up", True, True),)),
        ("yp", (("own", True, True), ("up", True, True), ("um", True, True))),
    ), "compare_near", ("um",))
    for_um, best = lax.optimization_barrier((move(for_um, -1, 0), best))
    best, for_uo, for_yp = compare(blocks, best, (
        ("own", (("uo", False, True),)),
        ("yp", (("uo", True, True),)),
    ), "compare_line", ("uo", "yp"))
    back = [for_um, move(for_uo, 2, 0), move(for_yp, 0, 1)]
    best, found, for_up, for_yo = compare(blocks, best, (
        ("yo", (("own", True, False), ("up", True, True), ("uo", False, True))),
    ), "compare_far", ("own", "up", "yo"))
    for_up, for_yo, *back = lax.optimization_barrier((for_up, for_yo, *back))
    back = back + [move(for_up, 1, 0), move(for_yo, 0, 2)]
    found = functools.reduce(jnp.maximum, back, found)
    kept = exchange(found)
    out = pl.pallas_call(
        finish_kernel, out_shape=jax.ShapeDtypeStruct((1, ROWS), jnp.float32), name="finish",
        in_specs=[VMEM] * 3, out_specs=VMEM,
        compiler_params=pltpu.CompilerParams(vmem_limit_bytes=8 * MIB),
    )(place, kept, swap(kept))
    return out.reshape(ROWS)


def solution(mesh):
    placed = (P(AXES, None), P(AXES, None), P(AXES))
    return jax.shard_map(
        per_device, mesh=mesh, in_specs=placed, out_specs=P(AXES), check_vma=False
    )
```
